512 devices in a mesh: node: 16 (over y_lo, x, core), ctx: 32 (over y_hi, z).
Axes of the slice: x: 4, y: 8 (y_hi: 4, y_lo: 2; y = y_hi * 2 + y_lo), z: 8, core: 2. Of those that a mesh axis runs over, the one named last changes fastest.
Arguments:
- block_order: int32 [64], replicated, may hold values from 0 to 63, each once
- query_states: bfloat16 [4096, 4096], P('ctx', 'node'), may hold values from -11 to 11, as said below
- key_states: bfloat16 [4096, 512], P('ctx'), may hold values from -12 to 12, as said below
- value_states: bfloat16 [4096, 512], P('ctx'), may hold values from -4 to 4
- out_weight: bfloat16 [4096, 5120], P(('node', 'ctx')), may hold values from -0.09375 to 0.09375
- out_grad: bfloat16 [4096, 5120], P('ctx', 'node'), may hold values from -5 to 5
Outputs:
- attention: bfloat16 [4096, 4096], P('ctx', 'node')
- query_grad: bfloat16 [4096, 4096], P('ctx', 'node')
- key_grad: bfloat16 [4096, 512], P('ctx', 'node')
- value_grad: bfloat16 [4096, 512], P('ctx', 'node')
- weight_grad: bfloat16 [4096, 5120], P(('node', 'ctx'))
The draws below stay inside these ranges and needn't reach their ends.
Inputs may be any that keep to these rules, and one draw needn't show every extreme that they name: `query_states`: entries are real numbers in the stated range. `key_states`: entries are real numbers in the stated range.
All inputs are finite; a program needn't handle non-finite values.
Results may differ from the reference program's by a relative error of at most 0.035.
Values may be sent and summed in bfloat16 or wider, within the bound.
A program may use at most 64 MiB of HBM per device.

```python
import math
import jax
import jax.numpy as jnp
from jax import lax

D = 5120
QH = 32
KVH = 4
HD = 128
TOK_DEV = 128
BLOCK = 64
BLOCKS = 64
TOKENS = 4096


def draw_query_states(key, part):
    key = jax.random.fold_in(key, 7)
    base_key, scale_key = jax.random.split(key)
    row_scale = jnp.exp(jax.random.uniform(scale_key, (TOKENS, QH, 1), jnp.float32, math.log(0.3), math.log(1.0)))
    values = jnp.clip(jax.random.normal(base_key, (TOKENS, QH, HD), jnp.float32), -4.0, 4.0) * row_scale
    return values.reshape(TOKENS, QH * HD).astype(jnp.bfloat16)


def draw_key_states(key, part):
    key = jax.random.fold_in(key, 13)
    base_key, scale_key = jax.random.split(key)
    row_scale = jnp.exp(jax.random.uniform(scale_key, (TOKENS, KVH, 1), jnp.float32, math.log(0.3), math.log(3.0)))
    values = jnp.clip(jax.random.normal(base_key, (TOKENS, KVH, HD), jnp.float32), -4.0, 4.0) * row_scale
    return values.reshape(TOKENS, KVH * HD).astype(jnp.bfloat16)


def block_scale(stream_key, dims, pieces, low, largest):
    loudness = 1.0
    for position, blocks in pieces:
        steps = jax.random.uniform(jax.random.fold_in(jax.random.fold_in(stream_key, 6), position), (blocks,), jnp.float32, low / len(pieces), largest / len(pieces))
        loudness = loudness * jnp.repeat(jnp.exp(steps), dims[position] // blocks).reshape((-1,) + (1,) * (len(dims) - 1 - position))
    return loudness


def scatter_about(rng, extent, spread, most, cuts=(), held_as=jnp.bfloat16):
    values = jax.random.normal(rng, extent, jnp.float32) * spread
    if len(cuts) > 0:
        values = block_scale(rng, extent, cuts, -0.22, 0.18) * values
    return jnp.clip(values, min=-most, max=most).astype(held_as)


def setup_inputs(seed: int = 0) -> dict:
    seeds = jax.random.split(jax.random.key(seed), 7)
    return {
        "block_order": jax.random.permutation(seeds[0], BLOCKS).astype(jnp.int32),
        "query_states": draw_query_states(jax.random.fold_in(seeds[6], 71), 0),
        "key_states": draw_key_states(jax.random.fold_in(seeds[6], 71), 0),
        "value_states": scatter_about(seeds[3], (TOKENS, KVH * HD), 1.0, 4.0, ((0, 32),)),
        "out_weight": scatter_about(seeds[4], (QH * HD, D), (QH * HD) ** -0.5, 0.09375, ((0, 512),)),
        "out_grad": scatter_about(seeds[5], (TOKENS, D), 1.0, 5.0, ((0, 32), (1, 16))),
    }


def positions(block_order):
    rows = jnp.arange(TOKENS, dtype=jnp.int32)
    return (block_order[rows // BLOCK] * BLOCK + rows % BLOCK).astype(jnp.int32)

def split_heads(matrix, head_count):
    return matrix.reshape(TOKENS, head_count, HD).transpose(1, 0, 2)

def merge_heads(stacked):
    return stacked.transpose(1, 0, 2).reshape(TOKENS, -1)

def reference(block_order, query_states, key_states, value_states, out_weight, out_grad):
    order = positions(block_order)
    allowed = order[None, :] <= order[:, None]
    score_scale = 1.0 / math.sqrt(HD)
    group_size = QH // KVH
    highest = lax.Precision.HIGHEST
    grad_attn = jnp.dot(out_grad, out_weight.T, preferred_element_type=jnp.float32).astype(jnp.bfloat16)
    query_heads = split_heads(query_states, QH)
    key_heads = jnp.repeat(split_heads(key_states, KVH), group_size, axis=0)
    value_heads = jnp.repeat(split_heads(value_states, KVH), group_size, axis=0)
    grad_heads = split_heads(grad_attn, QH)

    def one_head(operands):
        query_head, key_head, value_head, grad_head = operands
        scores = jnp.dot(query_head, key_head.T, preferred_element_type=jnp.float32) * score_scale
        row_max = lax.optimization_barrier(jnp.max(jnp.where(allowed, scores, -jnp.inf), axis=1, keepdims=True))
        total = lax.optimization_barrier(jnp.sum(jnp.where(allowed, jnp.exp(scores - row_max), 0.0), axis=1, keepdims=True))
        lse = row_max + jnp.log(total)
        softmax = jnp.where(allowed, jnp.exp(scores - lse), 0.0)
        attn_head = jnp.dot(softmax, value_head.astype(jnp.float32), precision=highest).astype(jnp.bfloat16)
        row_dot = lax.optimization_barrier(jnp.sum(grad_head.astype(jnp.float32) * attn_head.astype(jnp.float32), axis=1, keepdims=True))
        grad_probs = jnp.dot(grad_head, value_head.T, preferred_element_type=jnp.float32)
        grad_scores = softmax * (grad_probs - row_dot)
        query_part = (jnp.dot(grad_scores, key_head.astype(jnp.float32), precision=highest) * score_scale).astype(jnp.bfloat16)
        key_part = jnp.dot(grad_scores.T, query_head.astype(jnp.float32), precision=highest) * score_scale
        value_part = jnp.dot(softmax.T, grad_head.astype(jnp.float32), precision=highest)
        return (attn_head, query_part, key_part, value_part)
    attn_heads, query_parts, key_parts, value_parts = lax.map(one_head, (query_heads, key_heads, value_heads, grad_heads))
    attention = merge_heads(attn_heads)
    query_grad = merge_heads(query_parts)
    key_grad = merge_heads(key_parts.reshape(KVH, group_size, TOKENS, HD).sum(axis=1)).astype(jnp.bfloat16)
    value_grad = merge_heads(value_parts.reshape(KVH, group_size, TOKENS, HD).sum(axis=1)).astype(jnp.bfloat16)
    weight_sum = jnp.zeros((QH * HD, D), jnp.float32)
    for part_index in range(TOKENS // TOK_DEV):
        first_row = part_index * TOK_DEV
        partial_value = jnp.dot(attention[first_row:first_row + TOK_DEV].T, out_grad[first_row:first_row + TOK_DEV], preferred_element_type=jnp.float32).astype(jnp.bfloat16)
        partial_value = lax.optimization_barrier(partial_value)
        weight_sum = weight_sum + partial_value.astype(jnp.float32)
    weight_grad = weight_sum.astype(jnp.bfloat16)
    return (attention, query_grad, key_grad, value_grad, weight_grad)
```

```python
import functools
import math

import jax
import jax.numpy as jnp
from jax import lax
from jax.experimental import pallas as pl
from jax.experimental.pallas import tpu as pltpu
from jax.sharding import PartitionSpec as P

HD = 128
TOK = 128
NEG = -1e30
SCALE = 1.0 / math.sqrt(HD)
LOG2E = math.log2(math.e)
F32 = jnp.float32
BF16 = jnp.bfloat16
MESH = pl.DeviceIdType.MESH

OFFSET = (4, 5, 3, 6, 2, 7, 1, 0)
RIGHT_SLOT = (5, 3, 1, 0)
LEFT_SLOT = (6, 4, 2)


def nn(a, b):
    return lax.dot_general(a, b, (((1,), (0,)), ((), ())), preferred_element_type=F32)


def nt(a, b):
    return lax.dot_general(a, b, (((1,), (1,)), ((), ())), preferred_element_type=F32)


def fold8(a):
    return a.reshape(a.shape[0] // 8, 8, a.shape[1])


class Sems:
    def __init__(self, send, recv):
        self.send, self.recv, self.used = send, recv, 0

    def take(self, count):
        base = self.used
        self.used += count
        return base

    def copy(self, src, dst, sid, rid, node, ctx):
        return pltpu.make_async_remote_copy(
            src_ref=src,
            dst_ref=dst,
            send_sem=self.send.at[sid],
            recv_sem=self.recv.at[rid],
            device_id={"node": node, "ctx": ctx},
            device_id_type=MESH,
        )


SEM_COUNT = 96


def kernel(
    order_ref, q_ref, k_ref, v_ref, w_ref, og_ref,
    attn_ref, dq_ref, dk_ref, dv_ref, dw_ref,
    kvg, kv, qbuf, qall, krel, vrel, kt, vt,
    wsl, wring, w32, ogt, dot2,
    sp, mx, pb, dsb, mloc,
    osend, obuf, ostat, ostatbuf,
    at, gpart, gpsend, gpbuf, gown, gbuf, gstat, gstatbuf, gtall, frow, drow,
    smp, rsend_r, rsend_l, rrecv_r, rrecv_l, kvfin_send, kvfin,
    dqsend, dqbuf, dqown,
    dwp, wsend_r, wsend_l, wrecv_r, wrecv_l, dwsend, dwfin,
    send_sem, recv_sem,
):
    node = lax.axis_index("node")
    ctx = lax.axis_index("ctx")
    core = lax.rem(node, 2)
    x = lax.rem(node // 2, 4)
    ylo = node // 8
    g = node // 4
    m = lax.rem(node, 4)
    yhi = ctx // 8
    z = lax.rem(ctx, 8)

    sems = Sems(send_sem, recv_sem)
    pending = []

    def y_peer(k):
        return node, lax.rem(yhi + k, 4) * 8 + z

    def group_peer(k):
        return g * 4 + lax.rem(m + k, 4), ctx

    z_right = (node, yhi * 8 + lax.rem(z + 1, 8))
    z_left = (node, yhi * 8 + lax.rem(z + 7, 8))
    x_right = ((ylo * 4 + lax.rem(x + 1, 4)) * 2 + core, ctx)
    x_left = ((ylo * 4 + lax.rem(x + 3, 4)) * 2 + core, ctx)
    y_flip = (((1 - ylo) * 4 + x) * 2 + core, ctx)
    sibling = (node + 1 - 2 * core, ctx)
    turned = ((ylo * 4 + yhi) * 2 + core, x * 8 + z)

    barrier = pltpu.get_barrier_semaphore()

    def greet(peer):
        pl.semaphore_signal(
            barrier, inc=1, device_id={"node": peer[0], "ctx": peer[1]}, device_id_type=MESH
        )

    for k in range(1, 4):
        greet(y_peer(k))
        greet(group_peer(k))
    for peer in (z_right, z_left, x_right, x_left, y_flip):
        greet(peer)

    @pl.when(x != yhi)
    def _():
        greet(turned)

    @pl.when(m != yhi)
    def _():
        for k in range(1, 4):
            greet((g * 4 + yhi, lax.rem(yhi + k, 4) * 8 + z))

    glane = pl.ds(pl.multiple_of(g * HD, HD), HD)
    kvg[0] = k_ref[:, glane]
    kvg[1] = v_ref[:, glane]
    w_rows = w_ref[...].astype(F32)
    for q in range(4):
        slabs = []
        for j in range(10):
            col = 2560 * (j // 5) + 640 * q + 128 * (j % 5)
            slabs.append(w_rows[:, col : col + 128])
        wsl[q] = jnp.concatenate(slabs, axis=0).astype(BF16)
    eye = (
        lax.broadcasted_iota(jnp.int32, (320, 320), 0)
        == lax.broadcasted_iota(jnp.int32, (320, 320), 1)
    ).astype(F32).astype(BF16)
    ogt[...] = nt(eye, og_ref[...]).astype(BF16)

    pl.semaphore_wait(
        barrier, 11 + jnp.where(x != yhi, 1, 0) + jnp.where(m != yhi, 3, 0)
    )

    kv_hop = sems.take(4)
    kv_hop_copies = [
        sems.copy(kvg, kv.at[7], kv_hop + k, kv_hop, *y_peer(k)) for k in range(1, 4)
    ]

    @pl.when(m == yhi)
    def _():
        for copy in kv_hop_copies:
            copy.start()

    q_sem = sems.take(4)
    q_copies = [
        sems.copy(q_ref, qbuf.at[k], q_sem + k, q_sem + k, *group_peer(k)) for k in range(1, 4)
    ]
    for copy in q_copies:
        copy.start()
    pending += q_copies

    def dot_rows(lo, co):
        return pl.ds(pl.multiple_of((lo * 2 + co) * 320, 64), 320)

    def dot_lanes(position):
        return pl.ds(pl.multiple_of(position * TOK, TOK), TOK)

    turn_sem = sems.take(1)
    turn_copy = sems.copy(
        ogt, dot2.at[dot_rows(ylo, core), dot_lanes(yhi)], turn_sem, turn_sem, *turned
    )

    @pl.when(x != yhi)
    def _():
        turn_copy.start()

    @pl.when(x == yhi)
    def _():
        dot2[dot_rows(ylo, core), dot_lanes(yhi)] = ogt[...]

    w_sem = sems.take(4)
    w_copies = []
    for k in range(1, 4):
        peer = y_peer(k)
        w_copies.append(
            sems.copy(
                wsl.at[lax.rem(yhi + k, 4)], wring.at[7, yhi], w_sem + k, w_sem + k, *peer
            )
        )
        w_copies[-1].start()
    pending += w_copies
    wring[7, yhi] = wsl[yhi]

    def ring(buffer):
        base = sems.take(7)
        rights = [
            sems.copy(
                buffer.at[7 if s == 0 else RIGHT_SLOT[s - 1]],
                buffer.at[RIGHT_SLOT[s]],
                base + s,
                base + s,
                *z_right,
            )
            for s in range(4)
        ]
        lefts = [
            sems.copy(
                buffer.at[7 if s == 0 else LEFT_SLOT[s - 1]],
                buffer.at[LEFT_SLOT[s]],
                base + 4 + s,
                base + 4 + s,
                *z_left,
            )
            for s in range(3)
        ]
        return rights, lefts

    def ring_step(rings, s):
        rights, lefts = rings
        if s > 0:
            rights[s - 1].wait_recv()
            if s < 4:
                lefts[s - 1].wait_recv()
        if s < 4:
            rights[s].start()
            pending.append(rights[s])
        if s < 3:
            lefts[s].start()
            pending.append(lefts[s])

    kv_ring = ring(kv)
    w_ring = ring(wring)

    @pl.when(m == yhi)
    def _():
        kv[7] = kvg[...]

    @pl.when(m != yhi)
    def _():
        sems.copy(kvg, kv.at[7], kv_hop, kv_hop, *y_peer(1)).wait_recv()

    ring_step(kv_ring, 0)

    @pl.when(x != yhi)
    def _():
        turn_copy.wait_recv()

    flip_sem = sems.take(1)
    own_block = dot2.at[dot_rows(ylo, core), dot_lanes(x)]
    flip_copy = sems.copy(own_block, own_block, flip_sem, flip_sem, *y_flip)
    flip_copy.start()
    pending.append(flip_copy)

    for copy in w_copies:
        copy.wait_recv()
    ring_step(w_ring, 0)

    qbuf[0] = q_ref[...]
    for copy in q_copies:
        copy.wait_recv()
    for r in range(4):
        for h in range(2):
            qall[r * 256 + h * 128 : r * 256 + h * 128 + 128, :] = qbuf[
                r, :, h * 128 : h * 128 + 128
            ]

    def place(first_block, dim):
        index = lax.broadcasted_iota(jnp.int32, (TOK, TOK), dim)
        low = order_ref[first_block] * 64 + index
        high = order_ref[first_block + 1] * 64 + (index - 64)
        return jnp.where(index < 64, low, high)

    query_place = place(ctx * 2, 1)
    mx[...] = jnp.full(mx.shape, NEG, F32)

    def score_block(slot):
        block = m * 8 + lax.rem(z + OFFSET[slot], 8)
        allowed = place(block * 2, 0) <= query_place
        allowed = jnp.concatenate([allowed, allowed], axis=1)
        rows = slice(slot * 128, slot * 128 + 128)
        keys = kv[slot, 0]
        values = kv[slot, 1]
        krel[rows, :] = keys
        vrel[rows, :] = values
        kt[:, rows] = keys.astype(F32).T.astype(BF16)
        vt[:, rows] = values.astype(F32).T.astype(BF16)
        for r in range(4):
            lanes = slice(r * 256, r * 256 + 256)
            scores = nt(keys, qall[lanes, :]) * (SCALE * LOG2E)
            scores = jnp.where(allowed, scores, NEG)
            sp[rows, lanes] = scores
            mx[:, lanes] = jnp.maximum(mx[:, lanes], jnp.max(fold8(scores), axis=0))

    score_block(7)

    ring_step(kv_ring, 1)
    flip_copy.wait_recv()
    x_sem = sems.take(6)
    x_first = []
    for lo in range(2):
        block = dot2.at[dot_rows(lo, core), dot_lanes(x)]
        x_first.append(sems.copy(block, block, x_sem + lo, x_sem + lo, *x_right))
        x_first.append(sems.copy(block, block, x_sem + 2 + lo, x_sem + 2 + lo, *x_left))
    for copy in x_first:
        copy.start()
    pending += x_first
    score_block(5)
    score_block(6)
    ring_step(w_ring, 1)

    ring_step(kv_ring, 2)
    score_block(3)
    score_block(4)
    for copy in x_first:
        copy.wait_recv()
    from_left = dot2.at[dot_rows(0, core), dot_lanes(lax.rem(x + 3, 4))]
    from_right = dot2.at[dot_rows(1, core), dot_lanes(lax.rem(x + 1, 4))]
    x_second = [
        sems.copy(from_left, from_left, x_sem + 4, x_sem + 4, *x_right),
        sems.copy(from_right, from_right, x_sem + 5, x_sem + 5, *x_left),
    ]
    for copy in x_second:
        copy.start()
    pending += x_second
    ring_step(w_ring, 2)

    ring_step(kv_ring, 3)
    score_block(1)
    score_block(2)
    for copy in x_second:
        copy.wait_recv()
    core_sem = sems.take(2)
    core_copies = []
    for lo in range(2):
        half = dot2.at[dot_rows(lo, core), :]
        core_copies.append(sems.copy(half, half, core_sem + lo, core_sem + lo, *sibling))
        core_copies[-1].start()
    pending += core_copies
    ring_step(w_ring, 3)

    ring_step(kv_ring, 4)
    score_block(0)

    o_sem = sems.take(8)
    o_copies = []

    def forward(r):
        lanes = slice(r * 256, r * 256 + 256)
        row_max = jnp.maximum(jnp.max(mx[:, lanes], axis=0, keepdims=True), -1e20)

        def body(i, total):
            rows = pl.ds(pl.multiple_of(i * 128, 128), 128)
            weights = jnp.exp2(sp[rows, lanes] - row_max)
            sp[rows, lanes] = weights
            pb[rows, lanes] = weights.astype(BF16)
            return total + jnp.sum(fold8(weights), axis=0)

        total = lax.fori_loop(0, 8, body, jnp.zeros((8, 256), F32))
        row_sum = jnp.sum(total, axis=0, keepdims=True)
        mloc[:, lanes] = row_max
        return row_max, row_sum, nn(vt[...], pb[:, lanes])

    def stat_rows(first, second):
        index = lax.broadcasted_iota(jnp.int32, (8, 256), 0)
        return jnp.where(index == 0, first, second)

    for r in (1, 2, 3):
        row_max, row_sum, part = forward(r)
        osend[r] = part.astype(BF16)
        ostat[r] = stat_rows(row_max, row_sum)
        k = 4 - r
        peer = group_peer(k)
        o_copies.append(sems.copy(osend.at[r], obuf.at[k], o_sem + k, o_sem + k, *peer))
        o_copies.append(
            sems.copy(ostat.at[r], ostatbuf.at[k], o_sem + 4 + k, o_sem + 4 + k, *peer)
        )
        o_copies[-2].start()
        o_copies[-1].start()
    pending += o_copies
    own_max, own_sum, own_part = forward(0)
    obuf_own = own_part

    ring_step(w_ring, 4)
    for slot in range(8):
        first = lax.rem(z + OFFSET[slot], 8) * 8
        for y in range(4):
            block = wring[slot, y].astype(F32)
            rows = pl.ds(pl.multiple_of(first + y * 64, 8), 8)
            for j in range(10):
                w32[rows, j * 128 : j * 128 + 128] = block[j * 8 : j * 8 + 8, :]
    for copy in core_copies:
        copy.wait_recv()
    weight = w32[...].astype(BF16)
    gpart[...] = nn(weight, dot2[...])
    gp_sem = sems.take(4)
    gp_copies = []
    for k in range(1, 4):
        gpsend[k] = gpart[:, dot_lanes(lax.rem(yhi + k, 4))].astype(BF16)
        gp_copies.append(
            sems.copy(gpsend.at[k], gpbuf.at[k], gp_sem + k, gp_sem + k, *y_peer(k))
        )
        gp_copies[-1].start()
    pending += gp_copies

    for copy in o_copies:
        copy.wait_recv()
    maxes = [own_max] + [ostatbuf[k, 0:1, :] for k in range(1, 4)]
    sums = [own_sum] + [ostatbuf[k, 1:2, :] for k in range(1, 4)]
    parts = [obuf_own] + [obuf[k].astype(F32) for k in range(1, 4)]
    top = functools.reduce(jnp.maximum, maxes)
    factors = [jnp.exp2(value - top) for value in maxes]
    total = sum(f * s for f, s in zip(factors, sums))
    attention = sum(f * p for f, p in zip(factors, parts)) / total
    lse = top + jnp.log2(total)
    attention_rows = jnp.concatenate([attention[:, :128], attention[:, 128:]], axis=0)
    attention_bf = attention_rows.astype(BF16)
    my_lanes = dot_lanes(yhi)
    at[:, my_lanes] = attention_bf
    at_sem = sems.take(4)
    at_copies = []
    for k in range(1, 4):
        mine = at.at[:, my_lanes]
        at_copies.append(sems.copy(mine, mine, at_sem + k, at_sem + k, *y_peer(k)))
        at_copies[-1].start()
    pending += at_copies
    attn_ref[...] = attention_rows.T.astype(BF16)

    for copy in gp_copies:
        copy.wait_recv()
    grad = gpart[:, my_lanes]
    for k in range(1, 4):
        grad = grad + gpbuf[k].astype(F32)
    grad_bf = grad.astype(BF16)
    gown[...] = grad_bf
    products = grad_bf.astype(F32) * attention_bf.astype(F32)
    row_dot = jnp.concatenate(
        [
            jnp.sum(products[:128], axis=0, keepdims=True),
            jnp.sum(products[128:], axis=0, keepdims=True),
        ],
        axis=1,
    )
    own_stat = stat_rows(lse, row_dot)
    gstat[...] = own_stat
    g_sem = sems.take(8)
    g_copies = []
    for k in range(1, 4):
        peer = group_peer(k)
        g_copies.append(sems.copy(gown, gbuf.at[k], g_sem + k, g_sem + k, *peer))
        g_copies.append(
            sems.copy(gstat, gstatbuf.at[k], g_sem + 4 + k, g_sem + 4 + k, *peer)
        )
        g_copies[-2].start()
        g_copies[-1].start()
    pending += g_copies

    for copy in at_copies:
        copy.wait_recv()
    dwp[...] = nt(at[...], dot2[...])

    def weight_block(slot):
        first = lax.rem(z + OFFSET[slot], 8) * 8
        slabs = []
        for y in range(4):
            rows = pl.ds(pl.multiple_of(first + y * 64, 8), 8)
            for j in range(10):
                slabs.append(dwp[rows, j * 128 : j * 128 + 128])
        return jnp.concatenate(slabs, axis=0)

    def sum_ring(sends_r, recvs_r, sends_l, recvs_l):
        base = sems.take(7)
        rights = [
            sems.copy(sends_r.at[s], recvs_r.at[s], base + s, base + s, *z_right)
            for s in range(4)
        ]
        lefts = [
            sems.copy(sends_l.at[s], recvs_l.at[s], base + 4 + s, base + 4 + s, *z_left)
            for s in range(3)
        ]
        return rights, lefts

    dw_rights, dw_lefts = sum_ring(wsend_r, wrecv_r, wsend_l, wrecv_l)

    def weight_step(s):
        right = weight_block(2 * s)
        if s > 0:
            dw_rights[s - 1].wait_recv()
            right = right + wrecv_r[s - 1].astype(F32)
        wsend_r[s] = right.astype(BF16)
        dw_rights[s].start()
        pending.append(dw_rights[s])
        if s < 3:
            left = weight_block(2 * s + 1)
            if s > 0:
                dw_lefts[s - 1].wait_recv()
                left = left + wrecv_l[s - 1].astype(F32)
            wsend_l[s] = left.astype(BF16)
            dw_lefts[s].start()
            pending.append(dw_lefts[s])

    weight_step(0)

    for copy in g_copies:
        copy.wait_recv()
    for r in range(4):
        block = gown[...] if r == 0 else gbuf[r]
        for h in range(2):
            gtall[:, r * 256 + h * 128 : r * 256 + h * 128 + 128] = block[
                h * 128 : h * 128 + 128, :
            ]
        stat = own_stat if r == 0 else gstatbuf[r]
        lanes = slice(r * 256, r * 256 + 256)
        frow[:, lanes] = jnp.exp2(mloc[:, lanes] - stat[0:1, :])
        drow[:, lanes] = stat[1:2, :]

    kv_rights, kv_lefts = sum_ring(rsend_r, rrecv_r, rsend_l, rrecv_l)

    def backward(s):
        rows = slice(s * 256, s * 256 + 256)
        values = vrel[rows, :]
        for r in range(4):
            lanes = slice(r * 256, r * 256 + 256)
            grad_probs = nn(values, gtall[:, lanes])
            softmax = sp[rows, lanes] * frow[:, lanes]
            smp[:, lanes] = softmax.astype(BF16)
            dsb[rows, lanes] = (softmax * (grad_probs - drow[:, lanes])).astype(BF16)
        key_part = nn(dsb[rows, :], qall[...]) * SCALE
        value_part = nt(smp[...], gtall[...])
        return key_part, value_part

    own_key = own_value = None
    for s in range(4):
        key_part, value_part = backward(s)
        right_key, right_value = key_part[:128], value_part[:128]
        left_key, left_value = key_part[128:], value_part[128:]
        if s > 0:
            kv_rights[s - 1].wait_recv()
            right_key = right_key + rrecv_r[s - 1, 0].astype(F32)
            right_value = right_value + rrecv_r[s - 1, 1].astype(F32)
        rsend_r[s, 0] = right_key.astype(BF16)
        rsend_r[s, 1] = right_value.astype(BF16)
        kv_rights[s].start()
        pending.append(kv_rights[s])
        if s < 3:
            if s > 0:
                kv_lefts[s - 1].wait_recv()
                left_key = left_key + rrecv_l[s - 1, 0].astype(F32)
                left_value = left_value + rrecv_l[s - 1, 1].astype(F32)
            rsend_l[s, 0] = left_key.astype(BF16)
            rsend_l[s, 1] = left_value.astype(BF16)
            kv_lefts[s].start()
            pending.append(kv_lefts[s])
            weight_step(s + 1)
        else:
            own_key, own_value = left_key, left_value

    dq_sem = sems.take(4)
    dq_copies = []
    for r in (1, 2, 3, 0):
        lanes = slice(r * 256, r * 256 + 256)
        part = nn(kt[...], dsb[:, lanes]) * SCALE
        if r == 0:
            dqown[...] = part
        else:
            k = 4 - r
            dqsend[r] = part.astype(BF16)
            dq_copies.append(
                sems.copy(dqsend.at[r], dqbuf.at[k], dq_sem + k, dq_sem + k, *group_peer(k))
            )
            dq_copies[-1].start()
    pending += dq_copies

    kv_rights[3].wait_recv()
    kv_lefts[2].wait_recv()
    totals = []
    for i, own in ((0, own_key), (1, own_value)):
        total = own + rrecv_r[3, i].astype(F32) + rrecv_l[2, i].astype(F32)
        kvfin_send[i] = total.T.astype(BF16)
    fin_send = sems.take(4)
    fin_recv = sems.take(4)
    source = lax.rem(yhi - m + 4, 4)
    fin_copies = []
    for k in range(4):
        column = lax.rem(m + k, 4)
        fin_copies.append(
            sems.copy(
                kvfin_send.at[:, pl.ds(pl.multiple_of(column * 32, 32), 32), :],
                kvfin.at[source],
                fin_send + k,
                fin_recv + source,
                g * 4 + column,
                m * 8 + z,
            )
        )
    for k in range(1, 4):
        fin_copies[k].start()
        pending.append(fin_copies[k])

    @pl.when(m != yhi)
    def _():
        fin_copies[0].start()

    @pl.when(m == yhi)
    def _():
        kvfin[0] = kvfin_send[:, pl.ds(pl.multiple_of(m * 32, 32), 32), :]

    dw_rights[3].wait_recv()
    dw_lefts[2].wait_recv()
    total = weight_block(7) + wrecv_r[3].astype(F32) + wrecv_l[2].astype(F32)
    total = total.astype(BF16)
    for y in range(4):
        dwsend[y] = total[y * 80 : y * 80 + 80, :]
    dwf_sem = sems.take(4)
    dwf_copies = []
    for k in range(1, 4):
        dwf_copies.append(
            sems.copy(
                dwsend.at[lax.rem(yhi + k, 4)], dwfin.at[yhi], dwf_sem + k, dwf_sem + k, *y_peer(k)
            )
        )
        dwf_copies[-1].start()
    pending += dwf_copies
    dwfin[yhi] = dwsend[yhi]

    for copy in dq_copies:
        copy.wait_recv()
    query_grad = dqown[...]
    for k in range(1, 4):
        query_grad = query_grad + dqbuf[k].astype(F32)
    query_rows = jnp.concatenate([query_grad[:, :128], query_grad[:, 128:]], axis=0)
    dq_ref[...] = query_rows.T.astype(BF16)

    def fin_wait(s):
        sems.copy(
            kvfin_send.at[:, pl.ds(0, 32), :],
            kvfin.at[s],
            fin_send,
            fin_recv + s,
            *y_peer(1),
        ).wait_recv()

    for s in range(1, 4):
        fin_wait(s)

    @pl.when(m != yhi)
    def _():
        fin_wait(0)

    for i, out in ((0, dk_ref), (1, dv_ref)):
        total = kvfin[0, i].astype(F32)
        for s in range(1, 4):
            total = total + kvfin[s, i].astype(F32)
        square = jnp.concatenate([total, jnp.zeros((96, 128), F32)], axis=0).T
        out[...] = square[:, :32].astype(BF16)

    for copy in dwf_copies:
        copy.wait_recv()
    columns = []
    blocks = [dwfin[q].astype(F32) for q in range(4)]
    for lo in range(2):
        for q in range(4):
            for j in range(5):
                row = (lo * 5 + j) * 8
                columns.append(blocks[q][row : row + 8, :])
    dw_ref[...] = jnp.concatenate(columns, axis=1).astype(BF16)

    for copy in pending:
        copy.wait_send()

    @pl.when(m == yhi)
    def _():
        for copy in kv_hop_copies:
            copy.wait_send()

    @pl.when(x != yhi)
    def _():
        turn_copy.wait_send()

    @pl.when(m != yhi)
    def _():
        fin_copies[0].wait_send()

    assert sems.used <= SEM_COUNT, sems.used


def per_device(block_order, query_states, key_states, value_states, out_weight, out_grad):
    v = pltpu.VMEM
    vmem = pl.BlockSpec(memory_space=pltpu.VMEM)
    scratch = [
        v((2, 128, 128), BF16),
        v((8, 2, 128, 128), BF16),
        v((4, 128, 256), BF16),
        v((1024, 128), BF16),
        v((1024, 128), BF16),
        v((1024, 128), BF16),
        v((128, 1024), BF16),
        v((128, 1024), BF16),
        v((4, 80, 128), BF16),
        v((8, 4, 80, 128), BF16),
        v((256, 1280), F32),
        v((320, 128), BF16),
        v((1280, 512), BF16),
        v((1024, 1024), F32),
        v((8, 1024), F32),
        v((1024, 1024), BF16),
        v((1024, 1024), BF16),
        v((1, 1024), F32),
        v((4, 128, 256), BF16),
        v((4, 128, 256), BF16),
        v((4, 8, 256), F32),
        v((4, 8, 256), F32),
        v((256, 512), BF16),
        v((256, 512), F32),
        v((4, 256, 128), BF16),
        v((4, 256, 128), BF16),
        v((256, 128), BF16),
        v((4, 256, 128), BF16),
        v((8, 256), F32),
        v((4, 8, 256), F32),
        v((128, 1024), BF16),
        v((1, 1024), F32),
        v((1, 1024), F32),
        v((256, 1024), BF16),
        v((4, 2, 128, 128), BF16),
        v((3, 2, 128, 128), BF16),
        v((4, 2, 128, 128), BF16),
        v((3, 2, 128, 128), BF16),
        v((2, 128, 128), BF16),
        v((4, 2, 32, 128), BF16),
        v((4, 128, 256), BF16),
        v((4, 128, 256), BF16),
        v((128, 256), F32),
        v((256, 1280), F32),
        v((4, 320, 128), BF16),
        v((3, 320, 128), BF16),
        v((4, 320, 128), BF16),
        v((3, 320, 128), BF16),
        v((4, 80, 128), BF16),
        v((4, 80, 128), BF16),
        pltpu.SemaphoreType.DMA((SEM_COUNT,)),
        pltpu.SemaphoreType.DMA((SEM_COUNT,)),
    ]
    return pl.pallas_call(
        kernel,
        out_shape=(
            jax.ShapeDtypeStruct((128, 256), BF16),
            jax.ShapeDtypeStruct((128, 256), BF16),
            jax.ShapeDtypeStruct((128, 32), BF16),
            jax.ShapeDtypeStruct((128, 32), BF16),
            jax.ShapeDtypeStruct((8, 5120), BF16),
        ),
        in_specs=[pl.BlockSpec(memory_space=pltpu.SMEM)] + [vmem] * 5,
        out_specs=[vmem] * 5,
        scratch_shapes=scratch,
        compiler_params=pltpu.CompilerParams(
            collective_id=0, has_side_effects=True, vmem_limit_bytes=48 * 1024 * 1024
        ),
        cost_estimate=pl.CostEstimate(
            flops=2_500_000_000, bytes_accessed=1_000_000, transcendentals=1_100_000
        ),
    )(block_order, query_states, key_states, value_states, out_weight, out_grad)


def solution(mesh):
    in_specs = (
        P(),
        P("ctx", "node"),
        P("ctx", None),
        P("ctx", None),
        P(("node", "ctx"), None),
        P("ctx", "node"),
    )
    out_specs = (
        P("ctx", "node"),
        P("ctx", "node"),
        P("ctx", "node"),
        P("ctx", "node"),
        P(("node", "ctx"), None),
    )
    return jax.shard_map(
        per_device, mesh=mesh, in_specs=in_specs, out_specs=out_specs, check_vma=False
    )
```

```python
import functools
import math

import jax
import jax.numpy as jnp
from jax import lax
from jax.experimental import pallas as pl
from jax.experimental.pallas import tpu as pltpu
from jax.sharding import PartitionSpec as P

HD = 128
TOK = 128
NEG = -1e30
SCALE = 1.0 / math.sqrt(HD)
LOG2E = math.log2(math.e)
F32 = jnp.float32
BF16 = jnp.bfloat16
MESH = pl.DeviceIdType.MESH

OFFSET = (4, 5, 3, 6, 2, 7, 1, 0)
RIGHT_SLOT = (5, 3, 1, 0)
LEFT_SLOT = (6, 4, 2)


def nn(a, b):
    return lax.dot_general(a, b, (((1,), (0,)), ((), ())), preferred_element_type=F32)


def nt(a, b):
    return lax.dot_general(a, b, (((1,), (1,)), ((), ())), preferred_element_type=F32)


def fold8(a):
    return a.reshape(a.shape[0] // 8, 8, a.shape[1])


class Sems:
    def __init__(self, send, recv):
        self.send, self.recv, self.used = send, recv, 0

    def take(self, count):
        base = self.used
        self.used += count
        return base

    def copy(self, src, dst, sid, rid, node, ctx):
        return pltpu.make_async_remote_copy(
            src_ref=src,
            dst_ref=dst,
            send_sem=self.send.at[sid],
            recv_sem=self.recv.at[rid],
            device_id={"node": node, "ctx": ctx},
            device_id_type=MESH,
        )


SEM_COUNT = 128


def kernel(
    order_ref, q_ref, k_ref, v_ref, w_ref, og_ref,
    attn_ref, dq_ref, dk_ref, dv_ref, dw_ref,
    wv, kvg, kv, qbuf, qall, krel, vrel, kt, vt,
    wsl, wring, w32, ogt, dot2,
    sp, mx, pb, dsb, mloc,
    osend, obuf, ostat, ostatbuf,
    at, gpart, gpsend, gpfar, gpnear, gown, gbuf, gstat, gstatbuf, gtall, frow, drow,
    smp, rsend_r, rsend_l, rrecv_r, rrecv_l, kvfin_send, kvfin,
    dqsend, dqbuf, dqown,
    dwp, wsend_r, wsend_l, wrecv_r, wrecv_l, dwsend, dwfin,
    send_sem, recv_sem, load_sem,
):
    node = lax.axis_index("node")
    ctx = lax.axis_index("ctx")
    core = lax.rem(node, 2)
    x = lax.rem(node // 2, 4)
    ylo = node // 8
    g = node // 4
    quarter = ylo * 2 + core
    key_quarter = core * 2 + lax.rem(x, 2)
    m = lax.rem(node, 4)
    yhi = ctx // 8
    z = lax.rem(ctx, 8)

    sems = Sems(send_sem, recv_sem)
    pending = []

    def y_peer(k):
        return node, lax.rem(yhi + k, 4) * 8 + z

    def group_peer(k):
        return g * 4 + lax.rem(m + k, 4), ctx

    z_right = (node, yhi * 8 + lax.rem(z + 1, 8))
    z_left = (node, yhi * 8 + lax.rem(z + 7, 8))
    x_right = ((ylo * 4 + lax.rem(x + 1, 4)) * 2 + core, ctx)
    x_left = ((ylo * 4 + lax.rem(x + 3, 4)) * 2 + core, ctx)
    y_flip = (((1 - ylo) * 4 + x) * 2 + core, ctx)
    sibling = (node + 1 - 2 * core, ctx)
    turned = (((yhi // 2) * 4 + x) * 2 + lax.rem(yhi, 2), quarter * 8 + z)

    glane = pl.ds(pl.multiple_of(g * HD, HD), HD)
    loads = [
        pltpu.make_async_copy(og_ref, ogt, load_sem.at[0]),
        pltpu.make_async_copy(w_ref, wv, load_sem.at[1]),
        pltpu.make_async_copy(k_ref.at[:, glane], kvg.at[0], load_sem.at[2]),
        pltpu.make_async_copy(v_ref.at[:, glane], kvg.at[1], load_sem.at[3]),
        pltpu.make_async_copy(q_ref, qbuf.at[0], load_sem.at[4]),
    ]
    for load in loads:
        load.start()

    barrier = pltpu.get_barrier_semaphore()

    def greet(peer):
        pl.semaphore_signal(
            barrier, inc=1, device_id={"node": peer[0], "ctx": peer[1]}, device_id_type=MESH
        )

    for k in range(1, 4):
        greet(y_peer(k))
        greet(group_peer(k))
    for peer in (z_right, z_left, x_right, x_left, y_flip):
        greet(peer)

    @pl.when(quarter != yhi)
    def _():
        greet(turned)

    @pl.when(key_quarter != yhi)
    def _():
        for k in range(1, 4):
            greet((g * 4 + lax.rem(yhi, 2) * 2 + yhi // 2, lax.rem(yhi + k, 4) * 8 + z))

    loads[0].wait()
    low_half = lax.broadcasted_iota(jnp.int32, (8, 128), 1) < 64

    def join(a, b):
        return jnp.where(low_half, a, b)

    def turn(a):
        return pltpu.roll(a, 64, 1)

    loads[1].wait()
    w_rows = wv[...].astype(F32)
    for half in range(2):
        even, odd = [], []
        for pair in range(2):
            base = 20 * half + 10 * pair
            w = [w_rows[:, t * 128 : t * 128 + 128] for t in range(base, base + 10)]
            r = {t: turn(w[t]) for t in range(2, 8)}
            shifted = {t: join(r[t], r[t + 1]) for t in range(2, 7)}
            even += [w[0], w[1], join(w[2], shifted[4]), shifted[5], shifted[6]]
            odd += [shifted[2], shifted[3], join(shifted[4], w[7]), w[8], w[9]]
        wsl[2 * half] = jnp.concatenate(even, axis=0).astype(BF16)
        wsl[2 * half + 1] = jnp.concatenate(odd, axis=0).astype(BF16)
    for load in loads[2:]:
        load.wait()

    pl.semaphore_wait(
        barrier, 11 + jnp.where(quarter != yhi, 1, 0) + jnp.where(key_quarter != yhi, 3, 0)
    )

    kv_hop = sems.take(4)
    kv_hop_copies = [
        sems.copy(kvg, kv.at[7], kv_hop + k, kv_hop, *y_peer(k)) for k in range(1, 4)
    ]

    @pl.when(key_quarter == yhi)
    def _():
        for copy in kv_hop_copies:
            copy.start()

    def dot_rows(position):
        return pl.ds(pl.multiple_of(position * 320, 64), 320)

    def dot_lanes(position):
        return pl.ds(pl.multiple_of(position * TOK, TOK), TOK)

    turn_sem = sems.take(1)
    turn_copy = sems.copy(
        ogt, dot2.at[dot_rows(x), dot_lanes(yhi)], turn_sem, turn_sem, *turned
    )

    @pl.when(quarter != yhi)
    def _():
        turn_copy.start()

    @pl.when(quarter == yhi)
    def _():
        dot2[dot_rows(x), dot_lanes(yhi)] = ogt[...]

    w_sem = sems.take(4)
    w_copies = []
    for k in range(1, 4):
        peer = y_peer(k)
        w_copies.append(
            sems.copy(
                wsl.at[lax.rem(yhi + k, 4)], wring.at[7, yhi], w_sem + k, w_sem + k, *peer
            )
        )
        w_copies[-1].start()
    pending += w_copies
    wring[7, yhi] = wsl[yhi]

    q_sem = sems.take(4)
    q_copies = [
        sems.copy(qbuf.at[0], qbuf.at[k], q_sem + k, q_sem + k, *group_peer(k))
        for k in range(1, 4)
    ]
    for copy in q_copies:
        copy.start()
    pending += q_copies

    def ring(view):
        base = sems.take(7)
        rights = [
            sems.copy(
                view(7 if s == 0 else RIGHT_SLOT[s - 1]),
                view(RIGHT_SLOT[s]),
                base + s,
                base + s,
                *z_right,
            )
            for s in range(4)
        ]
        lefts = [
            sems.copy(
                view(7 if s == 0 else LEFT_SLOT[s - 1]),
                view(LEFT_SLOT[s]),
                base + 4 + s,
                base + 4 + s,
                *z_left,
            )
            for s in range(3)
        ]
        return rights, lefts

    def ring_step(rings, s):
        for rights, lefts in rings:
            if s > 0:
                rights[s - 1].wait_recv()
            if s < 4:
                rights[s].start()
                pending.append(rights[s])
            if 0 < s < 4:
                lefts[s - 1].wait_recv()
            if s < 3:
                lefts[s].start()
                pending.append(lefts[s])

    kv_ring = [ring(lambda slot, i=i: kv.at[slot, i]) for i in range(2)]
    w_ring = [ring(lambda slot, i=i: wring.at[slot, pl.ds(2 * i, 2)]) for i in range(2)]

    @pl.when(key_quarter == yhi)
    def _():
        kv[7] = kvg[...]

    @pl.when(key_quarter != yhi)
    def _():
        sems.copy(kvg, kv.at[7], kv_hop, kv_hop, *y_peer(1)).wait_recv()

    ring_step(kv_ring, 0)

    for copy in w_copies:
        copy.wait_recv()
    ring_step(w_ring, 0)

    @pl.when(quarter != yhi)
    def _():
        turn_copy.wait_recv()

    other_quarter = (1 - ylo) * 2 + core
    flip_sem = sems.take(1)
    own_block = dot2.at[dot_rows(x), dot_lanes(quarter)]
    flip_block = dot2.at[dot_rows(x), dot_lanes(other_quarter)]
    x_sem = sems.take(6)
    flip_copy = sems.copy(own_block, own_block, flip_sem, flip_sem, *y_flip)
    x_own = [
        sems.copy(own_block, own_block, x_sem, x_sem, *x_right),
        sems.copy(own_block, own_block, x_sem + 1, x_sem + 1, *x_left),
    ]
    x_flip = [
        sems.copy(flip_block, flip_block, x_sem + 2, x_sem + 2, *x_right),
        sems.copy(flip_block, flip_block, x_sem + 3, x_sem + 3, *x_left),
    ]
    for copy in [flip_copy] + x_own:
        copy.start()
        pending.append(copy)

    def unpack_weight(slot):
        first = lax.rem(z + OFFSET[slot], 8) * 8
        for y in range(4):
            block = wring[slot, y].astype(F32)
            rows = pl.ds(pl.multiple_of(first + y * 64, 8), 8)
            for j in range(10):
                w32[rows, j * 128 : j * 128 + 128] = block[j * 8 : j * 8 + 8, :]

    unpack_weight(7)

    for copy in q_copies:
        copy.wait_recv()
    for r in range(4):
        for h in range(2):
            qall[r * 256 + h * 128 : r * 256 + h * 128 + 128, :] = qbuf[
                r, :, h * 128 : h * 128 + 128
            ]

    def place(first_block, dim):
        index = lax.broadcasted_iota(jnp.int32, (TOK, TOK), dim)
        low = order_ref[first_block] * 64 + index
        high = order_ref[first_block + 1] * 64 + (index - 64)
        return jnp.where(index < 64, low, high)

    query_place = place(ctx * 2, 1)
    mx[...] = jnp.full(mx.shape, NEG, F32)

    def score_block(slot):
        block = key_quarter * 8 + lax.rem(z + OFFSET[slot], 8)
        allowed = place(block * 2, 0) <= query_place
        allowed = jnp.concatenate([allowed, allowed], axis=1)
        rows = slice(slot * 128, slot * 128 + 128)
        keys = kv[slot, 0]
        values = kv[slot, 1]
        krel[rows, :] = keys
        vrel[rows, :] = values
        kt[:, rows] = keys.astype(F32).T.astype(BF16)
        vt[:, rows] = values.astype(F32).T.astype(BF16)
        for r in range(4):
            lanes = slice(r * 256, r * 256 + 256)
            scores = nt(keys, qall[lanes, :]) * (SCALE * LOG2E)
            scores = jnp.where(allowed, scores, NEG)
            sp[rows, lanes] = scores
            mx[:, lanes] = jnp.maximum(mx[:, lanes], jnp.max(fold8(scores), axis=0))

    score_block(7)

    flip_copy.wait_recv()
    for copy in x_flip:
        copy.start()
    pending += x_flip
    ring_step(kv_ring, 1)
    ring_step(w_ring, 1)
    score_block(5)
    score_block(6)
    unpack_weight(5)
    unpack_weight(6)

    x_own[0].wait_recv()
    far_own = dot2.at[dot_rows(lax.rem(x + 3, 4)), dot_lanes(quarter)]
    x_far = [sems.copy(far_own, far_own, x_sem + 4, x_sem + 4, *x_right)]
    x_far[0].start()
    x_own[1].wait_recv()
    ring_step(kv_ring, 2)
    ring_step(w_ring, 2)
    score_block(3)
    score_block(4)
    unpack_weight(3)
    unpack_weight(4)
    x_flip[1].wait_recv()
    far_flip = dot2.at[dot_rows(lax.rem(x + 1, 4)), dot_lanes(other_quarter)]
    x_far.append(sems.copy(far_flip, far_flip, x_sem + 5, x_sem + 5, *x_left))
    x_far[1].start()
    x_flip[0].wait_recv()
    pending += x_far

    ring_step(kv_ring, 3)
    ring_step(w_ring, 3)
    score_block(1)
    score_block(2)
    unpack_weight(1)
    unpack_weight(2)
    for copy in x_far:
        copy.wait_recv()
    core_sem = sems.take(2)
    core_copies = []
    for i, position in enumerate((quarter, other_quarter)):
        half = dot2.at[:, dot_lanes(position)]
        core_copies.append(sems.copy(half, half, core_sem + i, core_sem + i, *sibling))
        core_copies[-1].start()
    pending += core_copies

    ring_step(kv_ring, 4)
    score_block(0)

    o_sem = sems.take(8)
    o_copies = []

    def forward(r):
        lanes = slice(r * 256, r * 256 + 256)
        row_max = jnp.maximum(jnp.max(mx[:, lanes], axis=0, keepdims=True), -1e20)

        def body(i, total):
            rows = pl.ds(pl.multiple_of(i * 128, 128), 128)
            weights = jnp.exp2(sp[rows, lanes] - row_max)
            sp[rows, lanes] = weights
            pb[rows, lanes] = weights.astype(BF16)
            return total + jnp.sum(fold8(weights), axis=0)

        total = lax.fori_loop(0, 8, body, jnp.zeros((8, 256), F32))
        row_sum = jnp.sum(total, axis=0, keepdims=True)
        mloc[:, lanes] = row_max
        return row_max, row_sum, nn(vt[...], pb[:, lanes])

    def stat_rows(first, second):
        index = lax.broadcasted_iota(jnp.int32, (8, 256), 0)
        return jnp.where(index == 0, first, second)

    for r in (2, 1, 3):
        row_max, row_sum, part = forward(r)
        osend[r] = part.astype(BF16)
        ostat[r] = stat_rows(row_max, row_sum)
        k = 4 - r
        peer = group_peer(k)
        o_copies.append(sems.copy(osend.at[r], obuf.at[k], o_sem + k, o_sem + k, *peer))
        o_copies.append(
            sems.copy(ostat.at[r], ostatbuf.at[k], o_sem + 4 + k, o_sem + 4 + k, *peer)
        )
        o_copies[-2].start()
        o_copies[-1].start()
    pending += o_copies
    ring_step(w_ring, 4)
    unpack_weight(0)
    weight = w32[...].astype(BF16)
    for copy in core_copies:
        copy.wait_recv()
    gpart[...] = nn(weight, dot2[...])
    heads = (slice(0, 128), slice(128, 256))
    lanes_of = [dot_lanes(lax.rem(yhi + k, 4)) for k in range(4)]
    gp_sem = sems.take(6)
    gp_far, gp_direct, gp_through = [], [], []
    for way, k in ((0, 1), (1, 3)):
        gpsend[way] = gpart[heads[way], lanes_of[2]].astype(BF16)
        gp_far.append(
            sems.copy(gpsend.at[way], gpfar.at[way], gp_sem + way, gp_sem + way, *y_peer(k))
        )
        gp_far[way].start()
    for way, k in ((0, 1), (1, 3)):
        gpsend[2 + way] = gpart[heads[1 - way], lanes_of[k]].astype(BF16)
        gp_direct.append(
            sems.copy(
                gpsend.at[2 + way], gpnear.at[way], gp_sem + 2 + way, gp_sem + 2 + way, *y_peer(k)
            )
        )
        gp_direct[way].start()
    pending += gp_far + gp_direct
    own_max, own_sum, own_part = forward(0)
    for way, k in ((0, 1), (1, 3)):
        gp_far[way].wait_recv()
        gpsend[4 + way] = (
            gpart[heads[way], lanes_of[k]] + gpfar[way].astype(F32)
        ).astype(BF16)
        gp_through.append(
            sems.copy(
                gpsend.at[4 + way],
                gpnear.at[2 + way],
                gp_sem + 4 + way,
                gp_sem + 4 + way,
                *y_peer(k),
            )
        )
        gp_through[way].start()
    pending += gp_through

    for copy in o_copies:
        copy.wait_recv()
    maxes = [own_max] + [ostatbuf[k, 0:1, :] for k in range(1, 4)]
    sums = [own_sum] + [ostatbuf[k, 1:2, :] for k in range(1, 4)]
    parts = [own_part] + [obuf[k].astype(F32) for k in range(1, 4)]
    top = functools.reduce(jnp.maximum, maxes)
    factors = [jnp.exp2(value - top) for value in maxes]
    total = sum(f * s for f, s in zip(factors, sums))
    attention = sum(f * p for f, p in zip(factors, parts)) / total
    lse = top + jnp.log2(total)
    attention_rows = jnp.concatenate([attention[:, :128], attention[:, 128:]], axis=0)
    attention_bf = attention_rows.astype(BF16)
    my_lanes = lanes_of[0]
    at[:, my_lanes] = attention_bf
    at_sem = sems.take(6)
    at_copies = []
    for way, k in ((0, 1), (1, 3)):
        for i, head in enumerate((way, 1 - way)):
            mine = at.at[heads[head], my_lanes]
            sem = at_sem + way * 2 + i
            at_copies.append(sems.copy(mine, mine, sem, sem, *y_peer(k)))
            at_copies[-1].start()
    pending += at_copies
    attn_ref[...] = attention_rows.T.astype(BF16)

    for copy in gp_direct + gp_through:
        copy.wait_recv()
    grad = gpart[:, my_lanes] + jnp.concatenate(
        [
            gpnear[1].astype(F32) + gpnear[2].astype(F32),
            gpnear[0].astype(F32) + gpnear[3].astype(F32),
        ],
        axis=0,
    )
    grad_bf = grad.astype(BF16)
    gown[...] = grad_bf
    products = grad_bf.astype(F32) * attention_bf.astype(F32)
    row_dot = jnp.concatenate(
        [
            jnp.sum(products[:128], axis=0, keepdims=True),
            jnp.sum(products[128:], axis=0, keepdims=True),
        ],
        axis=1,
    )
    own_stat = stat_rows(lse, row_dot)
    gstat[...] = own_stat
    g_sem = sems.take(8)
    g_copies = []
    for k in range(1, 4):
        peer = group_peer(k)
        g_copies.append(sems.copy(gown, gbuf.at[k], g_sem + k, g_sem + k, *peer))
        g_copies.append(
            sems.copy(gstat, gstatbuf.at[k], g_sem + 4 + k, g_sem + 4 + k, *peer)
        )
        g_copies[-2].start()
        g_copies[-1].start()
    pending += g_copies

    at_far = []
    for way, k in ((0, 1), (1, 3)):
        at_copies[2 * way].wait_recv()
        passed = at.at[heads[way], lanes_of[4 - k]]
        at_far.append(sems.copy(passed, passed, at_sem + 4 + way, at_sem + 4 + way, *y_peer(k)))
        at_far[way].start()
    pending += at_far

    def weight_block(slot, part):
        first = lax.rem(z + OFFSET[slot], 8) * 8
        slabs = []
        for y in (2 * part, 2 * part + 1):
            rows = pl.ds(pl.multiple_of(first + y * 64, 8), 8)
            for j in range(10):
                slabs.append(dwp[rows, j * 128 : j * 128 + 128])
        return jnp.concatenate(slabs, axis=0)

    def sum_ring(sends_r, recvs_r, sends_l, recvs_l):
        base = sems.take(7)
        rights = [
            sems.copy(sends_r.at[s], recvs_r.at[s], base + s, base + s, *z_right)
            for s in range(4)
        ]
        lefts = [
            sems.copy(sends_l.at[s], recvs_l.at[s], base + 4 + s, base + 4 + s, *z_left)
            for s in range(3)
        ]
        return rights, lefts

    dw_rings = [
        sum_ring(wsend_r.at[i], wrecv_r.at[i], wsend_l.at[i], wrecv_l.at[i]) for i in range(2)
    ]

    def weight_step(s):
        for i, (rights, lefts) in enumerate(dw_rings):
            right = weight_block(2 * s, i)
            if s > 0:
                rights[s - 1].wait_recv()
                right = right + wrecv_r[i, s - 1].astype(F32)
            wsend_r[i, s] = right.astype(BF16)
            rights[s].start()
            pending.append(rights[s])
            if s < 3:
                left = weight_block(2 * s + 1, i)
                if s > 0:
                    lefts[s - 1].wait_recv()
                    left = left + wrecv_l[i, s - 1].astype(F32)
                wsend_l[i, s] = left.astype(BF16)
                lefts[s].start()
                pending.append(lefts[s])

    for copy in g_copies:
        copy.wait_recv()
    for r in range(4):
        block = gown[...] if r == 0 else gbuf[r]
        for h in range(2):
            gtall[:, r * 256 + h * 128 : r * 256 + h * 128 + 128] = block[
                h * 128 : h * 128 + 128, :
            ]
        stat = own_stat if r == 0 else gstatbuf[r]
        lanes = slice(r * 256, r * 256 + 256)
        frow[:, lanes] = jnp.exp2(mloc[:, lanes] - stat[0:1, :])
        drow[:, lanes] = stat[1:2, :]

    kv_rights, kv_lefts = sum_ring(rsend_r, rrecv_r, rsend_l, rrecv_l)

    def backward(s):
        rows = slice(s * 256, s * 256 + 256)
        values = vrel[rows, :]
        for r in range(4):
            lanes = slice(r * 256, r * 256 + 256)
            grad_probs = nn(values, gtall[:, lanes])
            softmax = sp[rows, lanes] * frow[:, lanes]
            smp[:, lanes] = softmax.astype(BF16)
            dsb[rows, lanes] = (softmax * (grad_probs - drow[:, lanes])).astype(BF16)
        key_part = nn(dsb[rows, :], qall[...]) * SCALE
        value_part = nt(smp[...], gtall[...])
        return key_part, value_part

    own_key = own_value = None
    for s in range(4):
        key_part, value_part = backward(s)
        right_key, right_value = key_part[:128], value_part[:128]
        left_key, left_value = key_part[128:], value_part[128:]
        if s > 0:
            kv_rights[s - 1].wait_recv()
            right_key = right_key + rrecv_r[s - 1, 0].astype(F32)
            right_value = right_value + rrecv_r[s - 1, 1].astype(F32)
        rsend_r[s, 0] = right_key.astype(BF16)
        rsend_r[s, 1] = right_value.astype(BF16)
        kv_rights[s].start()
        pending.append(kv_rights[s])
        if s < 3:
            if s > 0:
                kv_lefts[s - 1].wait_recv()
                left_key = left_key + rrecv_l[s - 1, 0].astype(F32)
                left_value = left_value + rrecv_l[s - 1, 1].astype(F32)
            rsend_l[s, 0] = left_key.astype(BF16)
            rsend_l[s, 1] = left_value.astype(BF16)
            kv_lefts[s].start()
            pending.append(kv_lefts[s])
        else:
            own_key, own_value = left_key, left_value
        if s == 0:
            for copy in (at_copies[1], at_copies[3], at_far[0], at_far[1]):
                copy.wait_recv()
            dwp[...] = nt(at[...], dot2[...])
        weight_step(s)

    dq_sem = sems.take(4)
    dq_copies = []
    for r in (1, 2, 3, 0):
        lanes = slice(r * 256, r * 256 + 256)
        part = nn(kt[...], dsb[:, lanes]) * SCALE
        if r == 0:
            dqown[...] = part
        else:
            k = 4 - r
            dqsend[r] = part.astype(BF16)
            dq_copies.append(
                sems.copy(dqsend.at[r], dqbuf.at[k], dq_sem + k, dq_sem + k, *group_peer(k))
            )
            dq_copies[-1].start()
    pending += dq_copies

    kv_rights[3].wait_recv()
    kv_lefts[2].wait_recv()
    totals = []
    for i, own in ((0, own_key), (1, own_value)):
        total = own + rrecv_r[3, i].astype(F32) + rrecv_l[2, i].astype(F32)
        kvfin_send[i] = total.T.astype(BF16)
    fin_send = sems.take(4)
    fin_recv = sems.take(4)
    source = lax.rem(yhi - key_quarter + 4, 4)
    fin_copies = []
    for k in range(4):
        column = lax.rem(m + k, 4)
        fin_copies.append(
            sems.copy(
                kvfin_send.at[:, pl.ds(pl.multiple_of(column * 32, 32), 32), :],
                kvfin.at[source],
                fin_send + k,
                fin_recv + source,
                g * 4 + column,
                key_quarter * 8 + z,
            )
        )
    for k in range(1, 4):
        fin_copies[k].start()
        pending.append(fin_copies[k])

    @pl.when(key_quarter != yhi)
    def _():
        fin_copies[0].start()

    @pl.when(key_quarter == yhi)
    def _():
        kvfin[0] = kvfin_send[:, pl.ds(pl.multiple_of(m * 32, 32), 32), :]

    for i, (rights, lefts) in enumerate(dw_rings):
        rights[3].wait_recv()
        lefts[2].wait_recv()
        total = weight_block(7, i) + wrecv_r[i, 3].astype(F32) + wrecv_l[i, 2].astype(F32)
        total = total.astype(BF16)
        for y in range(2):
            dwsend[2 * i + y] = total[y * 80 : y * 80 + 80, :]
    dwf_sem = sems.take(4)
    dwf_copies = []
    for k in range(1, 4):
        dwf_copies.append(
            sems.copy(
                dwsend.at[lax.rem(yhi + k, 4)], dwfin.at[yhi], dwf_sem + k, dwf_sem + k, *y_peer(k)
            )
        )
        dwf_copies[-1].start()
    pending += dwf_copies
    dwfin[yhi] = dwsend[yhi]

    for copy in dq_copies:
        copy.wait_recv()
    query_grad = dqown[...]
    for k in range(1, 4):
        query_grad = query_grad + dqbuf[k].astype(F32)
    query_rows = jnp.concatenate([query_grad[:, :128], query_grad[:, 128:]], axis=0)
    dq_ref[...] = query_rows.T.astype(BF16)

    def fin_wait(s):
        sems.copy(
            kvfin_send.at[:, pl.ds(0, 32), :],
            kvfin.at[s],
            fin_send,
            fin_recv + s,
            *y_peer(1),
        ).wait_recv()

    for s in range(1, 4):
        fin_wait(s)

    @pl.when(key_quarter != yhi)
    def _():
        fin_wait(0)

    for i, out in ((0, dk_ref), (1, dv_ref)):
        total = kvfin[0, i].astype(F32)
        for s in range(1, 4):
            total = total + kvfin[s, i].astype(F32)
        out[...] = total.astype(BF16)

    for copy in dwf_copies:
        copy.wait_recv()
    columns = []
    blocks = [dwfin[q].astype(F32) for q in range(4)]
    for half in range(2):
        for pair in range(2):
            a, c = (
                [
                    blocks[2 * half + i][(pair * 5 + t) * 8 : (pair * 5 + t) * 8 + 8, :]
                    for t in range(5)
                ]
                for i in range(2)
            )
            columns += [
                a[0],
                a[1],
                join(a[2], turn(c[0])),
                join(turn(c[0]), turn(c[1])),
                join(turn(c[1]), turn(c[2])),
                join(turn(a[2]), turn(a[3])),
                join(turn(a[3]), turn(a[4])),
                join(turn(a[4]), c[2]),
                c[3],
                c[4],
            ]
    dw_ref[...] = jnp.concatenate(columns, axis=1).astype(BF16)

    for copy in pending:
        copy.wait_send()

    @pl.when(key_quarter == yhi)
    def _():
        for copy in kv_hop_copies:
            copy.wait_send()

    @pl.when(quarter != yhi)
    def _():
        turn_copy.wait_send()

    @pl.when(key_quarter != yhi)
    def _():
        fin_copies[0].wait_send()

    assert sems.used <= SEM_COUNT, sems.used


def deliver_kernel(*refs):
    count = len(refs) // 2
    for i in range(count):
        refs[count + i][...] = refs[i][...]


def deliver(results):
    vmem = pl.BlockSpec(memory_space=pltpu.VMEM)
    return pl.pallas_call(
        deliver_kernel,
        out_shape=[jax.ShapeDtypeStruct(r.shape, r.dtype) for r in results],
        in_specs=[vmem] * len(results),
        out_specs=[vmem] * len(results),
        compiler_params=pltpu.CompilerParams(vmem_limit_bytes=63 * 1024 * 1024),
    )(*results)


def per_device(block_order, query_states, key_states, value_states, out_weight, out_grad):
    v = pltpu.VMEM
    vmem = pl.BlockSpec(memory_space=pltpu.VMEM)
    scratch = [
        v((8, 5120), BF16),
        v((2, 128, 128), BF16),
        v((8, 2, 128, 128), BF16),
        v((4, 128, 256), BF16),
        v((1024, 128), BF16),
        v((1024, 128), BF16),
        v((1024, 128), BF16),
        v((128, 1024), BF16),
        v((128, 1024), BF16),
        v((4, 80, 128), BF16),
        v((8, 4, 80, 128), BF16),
        v((256, 1280), F32),
        v((320, 128), BF16),
        v((1280, 512), BF16),
        v((1024, 1024), F32),
        v((8, 1024), F32),
        v((1024, 1024), BF16),
        v((1024, 1024), BF16),
        v((1, 1024), F32),
        v((4, 128, 256), BF16),
        v((4, 128, 256), BF16),
        v((4, 8, 256), F32),
        v((4, 8, 256), F32),
        v((256, 512), BF16),
        v((256, 512), F32),
        v((6, 128, 128), BF16),
        v((2, 128, 128), BF16),
        v((4, 128, 128), BF16),
        v((256, 128), BF16),
        v((4, 256, 128), BF16),
        v((8, 256), F32),
        v((4, 8, 256), F32),
        v((128, 1024), BF16),
        v((1, 1024), F32),
        v((1, 1024), F32),
        v((256, 1024), BF16),
        v((4, 2, 128, 128), BF16),
        v((3, 2, 128, 128), BF16),
        v((4, 2, 128, 128), BF16),
        v((3, 2, 128, 128), BF16),
        v((2, 128, 128), BF16),
        v((4, 2, 32, 128), BF16),
        v((4, 128, 256), BF16),
        v((4, 128, 256), BF16),
        v((128, 256), F32),
        v((256, 1280), F32),
        v((2, 4, 160, 128), BF16),
        v((2, 3, 160, 128), BF16),
        v((2, 4, 160, 128), BF16),
        v((2, 3, 160, 128), BF16),
        v((4, 80, 128), BF16),
        v((4, 80, 128), BF16),
        pltpu.SemaphoreType.DMA((SEM_COUNT,)),
        pltpu.SemaphoreType.DMA((SEM_COUNT,)),
        pltpu.SemaphoreType.DMA((5,)),
    ]
    results = pl.pallas_call(
        kernel,
        out_shape=(
            jax.ShapeDtypeStruct((128, 256), BF16),
            jax.ShapeDtypeStruct((128, 256), BF16),
            jax.ShapeDtypeStruct((32, 128), BF16),
            jax.ShapeDtypeStruct((32, 128), BF16),
            jax.ShapeDtypeStruct((8, 5120), BF16),
        ),
        in_specs=[pl.BlockSpec(memory_space=pltpu.SMEM)] + [pl.BlockSpec(memory_space=pltpu.HBM)] * 5,
        out_specs=[vmem] * 5,
        scratch_shapes=scratch,
        compiler_params=pltpu.CompilerParams(
            collective_id=0, has_side_effects=True, vmem_limit_bytes=63 * 1024 * 1024
        ),
        cost_estimate=pl.CostEstimate(
            flops=2_500_000_000, bytes_accessed=1_000_000, transcendentals=1_100_000
        ),
    )(block_order, query_states, key_states, value_states, out_weight, out_grad.T)
    results = deliver(results)
    return results[0], results[1], results[2].T, results[3].T, results[4]


def solution(mesh):
    in_specs = (
        P(),
        P("ctx", "node"),
        P("ctx", None),
        P("ctx", None),
        P(("node", "ctx"), None),
        P("ctx", "node"),
    )
    out_specs = (
        P("ctx", "node"),
        P("ctx", "node"),
        P("ctx", "node"),
        P("ctx", "node"),
        P(("node", "ctx"), None),
    )
    return jax.shard_map(
        per_device, mesh=mesh, in_specs=in_specs, out_specs=out_specs, check_vma=False
    )
```

```python
import functools
import math

import jax
import jax.numpy as jnp
from jax import lax
from jax.experimental import pallas as pl
from jax.experimental.pallas import tpu as pltpu
from jax.sharding import PartitionSpec as P

HD = 128
TOK = 128
NEG = -1e30
SCALE = 1.0 / math.sqrt(HD)
LOG2E = math.log2(math.e)
F32 = jnp.float32
BF16 = jnp.bfloat16
MESH = pl.DeviceIdType.MESH

OFFSET = (4, 5, 3, 6, 2, 7, 1, 0)
RIGHT_SLOT = (5, 3, 1, 0)
LEFT_SLOT = (6, 4, 2, 0)
STEPS = ((4, 3), (3, 4))
RIGHT_SUM = ((0, 2, 4, 6), (2, 4, 6))
LEFT_SUM = ((1, 3, 5), (0, 1, 3, 5))


def nn(a, b):
    return lax.dot_general(a, b, (((1,), (0,)), ((), ())), preferred_element_type=F32)


def nt(a, b):
    return lax.dot_general(a, b, (((1,), (1,)), ((), ())), preferred_element_type=F32)


def fold8(a):
    return a.reshape(a.shape[0] // 8, 8, a.shape[1])


class Sems:
    def __init__(self, send, recv):
        self.send, self.recv, self.used = send, recv, 0

    def take(self, count):
        base = self.used
        self.used += count
        return base

    def copy(self, src, dst, sid, rid, node, ctx):
        return pltpu.make_async_remote_copy(
            src_ref=src,
            dst_ref=dst,
            send_sem=self.send.at[sid],
            recv_sem=self.recv.at[rid],
            device_id={"node": node, "ctx": ctx},
            device_id_type=MESH,
        )


SEM_COUNT = 128


def kernel(
    order_ref, q_ref, k_ref, v_ref, w_ref, og_ref,
    attn_ref, dq_ref, dk_ref, dv_ref, dw_ref,
    wv, kvg, kv, qbuf, qall, krel, vrel, kt, vt,
    wsl, wring, w32, ogt, dot2,
    sp, mx, pb, dsb, mloc,
    osend, obuf, ostat, ostatbuf,
    at, gpart, gpsend, gpfar, gpnear, gown, gbuf, gstat, gstatbuf, gtall, frow, drow,
    smp, kvpart, rsend, rrecv, kvfin_send, kvfin,
    dqsend, dqbuf, dqown,
    dwp, wsend, wrecv, dwsend, dwfin,
    send_sem, recv_sem, load_sem,
):
    node = lax.axis_index("node")
    ctx = lax.axis_index("ctx")
    core = lax.rem(node, 2)
    x = lax.rem(node // 2, 4)
    ylo = node // 8
    g = node // 4
    quarter = ylo * 2 + core
    key_quarter = core * 2 + lax.rem(x, 2)
    m = lax.rem(node, 4)
    yhi = ctx // 8
    z = lax.rem(ctx, 8)

    sems = Sems(send_sem, recv_sem)
    pending = []

    def y_peer(k):
        return node, lax.rem(yhi + k, 4) * 8 + z

    def group_peer(k):
        return g * 4 + lax.rem(m + k, 4), ctx

    z_right = (node, yhi * 8 + lax.rem(z + 1, 8))
    z_left = (node, yhi * 8 + lax.rem(z + 7, 8))
    x_right = ((ylo * 4 + lax.rem(x + 1, 4)) * 2 + core, ctx)
    x_left = ((ylo * 4 + lax.rem(x + 3, 4)) * 2 + core, ctx)
    y_flip = (((1 - ylo) * 4 + x) * 2 + core, ctx)
    sibling = (node + 1 - 2 * core, ctx)
    turned = (((yhi // 2) * 4 + x) * 2 + lax.rem(yhi, 2), quarter * 8 + z)

    glane = pl.ds(pl.multiple_of(g * HD, HD), HD)
    loads = [
        pltpu.make_async_copy(og_ref, ogt, load_sem.at[0]),
        pltpu.make_async_copy(w_ref, wv, load_sem.at[1]),
        pltpu.make_async_copy(k_ref.at[:, glane], kvg.at[0], load_sem.at[2]),
        pltpu.make_async_copy(v_ref.at[:, glane], kvg.at[1], load_sem.at[3]),
        pltpu.make_async_copy(q_ref, qbuf.at[0], load_sem.at[4]),
    ]
    for load in loads:
        load.start()

    barrier = pltpu.get_barrier_semaphore()

    def greet(peer):
        pl.semaphore_signal(
            barrier, inc=1, device_id={"node": peer[0], "ctx": peer[1]}, device_id_type=MESH
        )

    for k in range(1, 4):
        greet(y_peer(k))
        greet(group_peer(k))
    for peer in (z_right, z_left, x_right, x_left, y_flip):
        greet(peer)

    @pl.when(quarter != yhi)
    def _():
        greet(turned)

    @pl.when(key_quarter != yhi)
    def _():
        for k in range(1, 4):
            greet((g * 4 + lax.rem(yhi, 2) * 2 + yhi // 2, lax.rem(yhi + k, 4) * 8 + z))

    loads[0].wait()
    low_half = lax.broadcasted_iota(jnp.int32, (8, 128), 1) < 64

    def join(a, b):
        return jnp.where(low_half, a, b)

    def turn(a):
        return pltpu.roll(a, 64, 1)

    loads[1].wait()
    w_rows = wv[...].astype(F32)
    for half in range(2):
        even, odd = [], []
        for pair in range(2):
            base = 20 * half + 10 * pair
            w = [w_rows[:, t * 128 : t * 128 + 128] for t in range(base, base + 10)]
            r = {t: turn(w[t]) for t in range(2, 8)}
            shifted = {t: join(r[t], r[t + 1]) for t in range(2, 7)}
            even += [w[0], w[1], join(w[2], shifted[4]), shifted[5], shifted[6]]
            odd += [shifted[2], shifted[3], join(shifted[4], w[7]), w[8], w[9]]
        wsl[2 * half] = jnp.concatenate(even, axis=0).astype(BF16)
        wsl[2 * half + 1] = jnp.concatenate(odd, axis=0).astype(BF16)
    for load in loads[2:]:
        load.wait()

    pl.semaphore_wait(
        barrier, 11 + jnp.where(quarter != yhi, 1, 0) + jnp.where(key_quarter != yhi, 3, 0)
    )

    def dot_rows(position):
        return pl.ds(pl.multiple_of(position * 320, 64), 320)

    def dot_lanes(position):
        return pl.ds(pl.multiple_of(position * TOK, TOK), TOK)

    turn_sem = sems.take(1)
    turn_copy = sems.copy(
        ogt, dot2.at[dot_rows(x), dot_lanes(yhi)], turn_sem, turn_sem, *turned
    )

    @pl.when(quarter != yhi)
    def _():
        turn_copy.start()

    @pl.when(quarter == yhi)
    def _():
        dot2[dot_rows(x), dot_lanes(yhi)] = ogt[...]

    w_sem = sems.take(4)
    w_copies = []
    for k in range(1, 4):
        peer = y_peer(k)
        w_copies.append(
            sems.copy(
                wsl.at[lax.rem(yhi + k, 4)], wring.at[7, yhi], w_sem + k, w_sem + k, *peer
            )
        )
        w_copies[-1].start()
    pending += w_copies
    wring[7, yhi] = wsl[yhi]

    kv_hop = sems.take(4)
    kv_hop_copies = [
        sems.copy(kvg, kv.at[7], kv_hop + k, kv_hop, *y_peer(k)) for k in range(1, 4)
    ]

    @pl.when(key_quarter == yhi)
    def _():
        for copy in kv_hop_copies:
            copy.start()

    q_sem = sems.take(4)
    q_copies = [
        sems.copy(qbuf.at[0], qbuf.at[k], q_sem + k, q_sem + k, *group_peer(k))
        for k in range(1, 4)
    ]
    for copy in q_copies:
        copy.start()
    pending += q_copies

    def ring(half, view):
        base = sems.take(7)
        ways = []
        for count, slots, peer in zip(STEPS[half], (RIGHT_SLOT, LEFT_SLOT), (z_right, z_left)):
            ways.append(
                [
                    sems.copy(
                        view(7 if s == 0 else slots[s - 1]),
                        view(slots[s]),
                        base + s,
                        base + s,
                        *peer,
                    )
                    for s in range(count)
                ]
            )
            base += count
        return ways

    def ring_step(rings, s):
        for ways in rings:
            for copies in ways:
                if 0 < s <= len(copies):
                    copies[s - 1].wait_recv()
                if s < len(copies):
                    copies[s].start()
                    pending.append(copies[s])

    kv_ring = [ring(i, lambda slot, i=i: kv.at[slot, i]) for i in range(2)]
    w_ring = [ring(i, lambda slot, i=i: wring.at[slot, pl.ds(2 * i, 2)]) for i in range(2)]

    @pl.when(quarter != yhi)
    def _():
        turn_copy.wait_recv()

    other_quarter = (1 - ylo) * 2 + core
    flip_sem = sems.take(1)
    own_block = dot2.at[dot_rows(x), dot_lanes(quarter)]
    flip_block = dot2.at[dot_rows(x), dot_lanes(other_quarter)]
    x_sem = sems.take(6)
    flip_copy = sems.copy(own_block, own_block, flip_sem, flip_sem, *y_flip)
    x_own = [
        sems.copy(own_block, own_block, x_sem, x_sem, *x_right),
        sems.copy(own_block, own_block, x_sem + 1, x_sem + 1, *x_left),
    ]
    x_flip = [
        sems.copy(flip_block, flip_block, x_sem + 2, x_sem + 2, *x_right),
        sems.copy(flip_block, flip_block, x_sem + 3, x_sem + 3, *x_left),
    ]
    for copy in [flip_copy] + x_own:
        copy.start()
        pending.append(copy)

    core_sem = sems.take(8)
    core_copies = []

    def share(row_position, lane_position):
        block = dot2.at[dot_rows(row_position), dot_lanes(lane_position)]
        sem = core_sem + len(core_copies)
        core_copies.append(sems.copy(block, block, sem, sem, *sibling))
        core_copies[-1].start()
        pending.append(core_copies[-1])

    share(x, quarter)

    for copy in w_copies:
        copy.wait_recv()
    ring_step(w_ring, 0)

    @pl.when(key_quarter == yhi)
    def _():
        kv[7] = kvg[...]

    @pl.when(key_quarter != yhi)
    def _():
        sems.copy(kvg, kv.at[7], kv_hop, kv_hop, *y_peer(1)).wait_recv()

    ring_step(kv_ring, 0)

    def unpack_weight(slot):
        first = lax.rem(z + OFFSET[slot], 8) * 8
        for y in range(4):
            block = wring[slot, y].astype(F32)
            rows = pl.ds(pl.multiple_of(first + y * 64, 8), 8)
            for j in range(10):
                w32[rows, j * 128 : j * 128 + 128] = block[j * 8 : j * 8 + 8, :]

    unpack_weight(7)

    for copy in q_copies:
        copy.wait_recv()
    for r in range(4):
        for h in range(2):
            qall[r * 256 + h * 128 : r * 256 + h * 128 + 128, :] = qbuf[
                r, :, h * 128 : h * 128 + 128
            ]

    def place(first_block, dim):
        index = lax.broadcasted_iota(jnp.int32, (TOK, TOK), dim)
        low = order_ref[first_block] * 64 + index
        high = order_ref[first_block + 1] * 64 + (index - 64)
        return jnp.where(index < 64, low, high)

    query_place = place(ctx * 2, 1)
    mx[...] = jnp.full(mx.shape, NEG, F32)

    def score_block(slot):
        block = key_quarter * 8 + lax.rem(z + OFFSET[slot], 8)
        allowed = place(block * 2, 0) <= query_place
        allowed = jnp.concatenate([allowed, allowed], axis=1)
        rows = slice(slot * 128, slot * 128 + 128)
        keys = kv[slot, 0]
        values = kv[slot, 1]
        krel[rows, :] = keys
        vrel[rows, :] = values
        kt[:, rows] = keys.astype(F32).T.astype(BF16)
        vt[:, rows] = values.astype(F32).T.astype(BF16)
        for r in range(4):
            lanes = slice(r * 256, r * 256 + 256)
            scores = nt(keys, qall[lanes, :]) * (SCALE * LOG2E)
            scores = jnp.where(allowed, scores, NEG)
            sp[rows, lanes] = scores
            mx[:, lanes] = jnp.maximum(mx[:, lanes], jnp.max(fold8(scores), axis=0))

    score_block(7)

    flip_copy.wait_recv()
    for copy in x_flip:
        copy.start()
    pending += x_flip
    share(x, other_quarter)
    ring_step(w_ring, 1)
    ring_step(kv_ring, 1)
    score_block(5)
    score_block(6)
    unpack_weight(5)
    unpack_weight(6)

    x_own[0].wait_recv()
    far_own = dot2.at[dot_rows(lax.rem(x + 3, 4)), dot_lanes(quarter)]
    x_far = [sems.copy(far_own, far_own, x_sem + 4, x_sem + 4, *x_right)]
    x_far[0].start()
    x_own[1].wait_recv()
    share(lax.rem(x + 3, 4), quarter)
    share(lax.rem(x + 1, 4), quarter)
    ring_step(w_ring, 2)
    ring_step(kv_ring, 2)
    score_block(3)
    score_block(4)
    unpack_weight(3)
    unpack_weight(4)
    x_flip[1].wait_recv()
    far_flip = dot2.at[dot_rows(lax.rem(x + 1, 4)), dot_lanes(other_quarter)]
    x_far.append(sems.copy(far_flip, far_flip, x_sem + 5, x_sem + 5, *x_left))
    x_far[1].start()
    x_flip[0].wait_recv()
    share(lax.rem(x + 3, 4), other_quarter)
    share(lax.rem(x + 1, 4), other_quarter)
    pending += x_far

    ring_step(w_ring, 3)
    ring_step(kv_ring, 3)
    score_block(1)
    score_block(2)
    unpack_weight(1)
    unpack_weight(2)
    for copy in x_far:
        copy.wait_recv()
    share(lax.rem(x + 2, 4), quarter)
    share(lax.rem(x + 2, 4), other_quarter)

    ring_step(w_ring, 4)
    unpack_weight(0)
    weight = w32[...].astype(BF16)
    for copy in core_copies:
        copy.wait_recv()
    gpart[...] = nn(weight, dot2[...])
    heads = (slice(0, 128), slice(128, 256))
    lanes_of = [dot_lanes(lax.rem(yhi + k, 4)) for k in range(4)]
    my_lanes = lanes_of[0]
    gp_sem = sems.take(6)
    gp_far, gp_direct, gp_through = [], [], []
    for way, k in ((0, 1), (1, 3)):
        gpsend[way] = gpart[heads[way], lanes_of[2]].astype(BF16)
        gp_far.append(
            sems.copy(gpsend.at[way], gpfar.at[way], gp_sem + way, gp_sem + way, *y_peer(k))
        )
        gp_far[way].start()
    for way, k in ((0, 1), (1, 3)):
        gpsend[2 + way] = gpart[heads[1 - way], lanes_of[k]].astype(BF16)
        gp_direct.append(
            sems.copy(
                gpsend.at[2 + way], gpnear.at[way], gp_sem + 2 + way, gp_sem + 2 + way, *y_peer(k)
            )
        )
        gp_direct[way].start()
    pending += gp_far + gp_direct
    ring_step(kv_ring, 4)
    score_block(0)

    o_sem = sems.take(8)
    o_copies = []

    def forward(r):
        lanes = slice(r * 256, r * 256 + 256)
        row_max = jnp.maximum(jnp.max(mx[:, lanes], axis=0, keepdims=True), -1e20)

        def body(i, total):
            rows = pl.ds(pl.multiple_of(i * 128, 128), 128)
            weights = jnp.exp2(sp[rows, lanes] - row_max)
            sp[rows, lanes] = weights
            pb[rows, lanes] = weights.astype(BF16)
            return total + jnp.sum(fold8(weights), axis=0)

        total = lax.fori_loop(0, 8, body, jnp.zeros((8, 256), F32))
        row_sum = jnp.sum(total, axis=0, keepdims=True)
        mloc[:, lanes] = row_max
        return row_max, row_sum, nn(vt[...], pb[:, lanes])

    def stat_rows(first, second):
        index = lax.broadcasted_iota(jnp.int32, (8, 256), 0)
        return jnp.where(index == 0, first, second)

    for r in (2, 1, 3):
        row_max, row_sum, part = forward(r)
        osend[r] = part.astype(BF16)
        ostat[r] = stat_rows(row_max, row_sum)
        k = 4 - r
        peer = group_peer(k)
        o_copies.append(sems.copy(osend.at[r], obuf.at[k], o_sem + k, o_sem + k, *peer))
        o_copies.append(
            sems.copy(ostat.at[r], ostatbuf.at[k], o_sem + 4 + k, o_sem + 4 + k, *peer)
        )
        o_copies[-2].start()
        o_copies[-1].start()
    pending += o_copies
    for way, k in ((0, 1), (1, 3)):
        gp_far[way].wait_recv()
        gpsend[4 + way] = (
            gpart[heads[way], lanes_of[k]] + gpfar[way].astype(F32)
        ).astype(BF16)
        gp_through.append(
            sems.copy(
                gpsend.at[4 + way],
                gpnear.at[2 + way],
                gp_sem + 4 + way,
                gp_sem + 4 + way,
                *y_peer(k),
            )
        )
        gp_through[way].start()
    pending += gp_through

    own_max, own_sum, own_part = forward(0)

    for copy in gp_direct + gp_through:
        copy.wait_recv()
    grad = gpart[:, my_lanes] + jnp.concatenate(
        [
            gpnear[1].astype(F32) + gpnear[2].astype(F32),
            gpnear[0].astype(F32) + gpnear[3].astype(F32),
        ],
        axis=0,
    )
    grad_bf = grad.astype(BF16)
    gown[...] = grad_bf
    g_sem = sems.take(8)
    g_copies = []
    for k in range(1, 4):
        g_copies.append(sems.copy(gown, gbuf.at[k], g_sem + k, g_sem + k, *group_peer(k)))
        g_copies[-1].start()

    for copy in o_copies:
        copy.wait_recv()
    maxes = [own_max] + [ostatbuf[k, 0:1, :] for k in range(1, 4)]
    sums = [own_sum] + [ostatbuf[k, 1:2, :] for k in range(1, 4)]
    parts = [own_part] + [obuf[k].astype(F32) for k in range(1, 4)]
    top = functools.reduce(jnp.maximum, maxes)
    factors = [jnp.exp2(value - top) for value in maxes]
    total = sum(f * s for f, s in zip(factors, sums))
    attention = sum(f * p for f, p in zip(factors, parts)) / total
    lse = top + jnp.log2(total)
    attention_rows = jnp.concatenate([attention[:, :128], attention[:, 128:]], axis=0)
    attention_bf = attention_rows.astype(BF16)
    at[:, my_lanes] = attention_bf
    at_sem = sems.take(6)
    at_copies = []
    for way, k in ((0, 1), (1, 3)):
        for i, head in enumerate((way, 1 - way)):
            mine = at.at[heads[head], my_lanes]
            sem = at_sem + way * 2 + i
            at_copies.append(sems.copy(mine, mine, sem, sem, *y_peer(k)))
            at_copies[-1].start()
    pending += at_copies
    products = grad_bf.astype(F32) * attention_bf.astype(F32)
    row_dot = jnp.concatenate(
        [
            jnp.sum(products[:128], axis=0, keepdims=True),
            jnp.sum(products[128:], axis=0, keepdims=True),
        ],
        axis=1,
    )
    own_stat = stat_rows(lse, row_dot)
    gstat[...] = own_stat
    for k in range(1, 4):
        g_copies.append(
            sems.copy(gstat, gstatbuf.at[k], g_sem + 4 + k, g_sem + 4 + k, *group_peer(k))
        )
        g_copies[-1].start()
    pending += g_copies

    attn_ref[...] = attention_rows.T.astype(BF16)
    at_far = []
    for way, k in ((0, 1), (1, 3)):
        at_copies[2 * way].wait_recv()
        passed = at.at[heads[way], lanes_of[4 - k]]
        at_far.append(sems.copy(passed, passed, at_sem + 4 + way, at_sem + 4 + way, *y_peer(k)))
        at_far[way].start()
    pending += at_far

    def weight_block(slot, part):
        first = lax.rem(z + OFFSET[slot], 8) * 8
        slabs = []
        for y in (2 * part, 2 * part + 1):
            rows = pl.ds(pl.multiple_of(first + y * 64, 8), 8)
            for j in range(10):
                slabs.append(dwp[rows, j * 128 : j * 128 + 128])
        return jnp.concatenate(slabs, axis=0)

    def sum_ring(half, block, sends, recvs):
        base = sems.take(7)
        ways = []
        for way, (slots, peer) in enumerate(((RIGHT_SUM, z_right), (LEFT_SUM, z_left))):
            slots = slots[half]
            ways.append(
                (
                    way,
                    slots,
                    [
                        sems.copy(
                            sends.at[half, way, s],
                            recvs.at[half, way, s],
                            base + s,
                            base + s,
                            *peer,
                        )
                        for s in range(len(slots))
                    ],
                )
            )
            base += len(slots)

        def step(s):
            for way, slots, copies in ways:
                if s < len(slots):
                    value = block(slots[s])
                    if s > 0:
                        copies[s - 1].wait_recv()
                        value = value + recvs[half, way, s - 1].astype(F32)
                    sends[half, way, s] = value.astype(BF16)
                    copies[s].start()
                    pending.append(copies[s])

        def finish():
            total = block(7)
            for way, slots, copies in ways:
                copies[-1].wait_recv()
                total = total + recvs[half, way, len(slots) - 1].astype(F32)
            return total

        return step, finish

    dw_rings = [
        sum_ring(i, lambda slot, i=i: weight_block(slot, i), wsend, wrecv) for i in range(2)
    ]

    for copy in g_copies:
        copy.wait_recv()
    for r in range(4):
        block = gown[...] if r == 0 else gbuf[r]
        for h in range(2):
            gtall[:, r * 256 + h * 128 : r * 256 + h * 128 + 128] = block[
                h * 128 : h * 128 + 128, :
            ]
        stat = own_stat if r == 0 else gstatbuf[r]
        lanes = slice(r * 256, r * 256 + 256)
        frow[:, lanes] = jnp.exp2(mloc[:, lanes] - stat[0:1, :])
        drow[:, lanes] = stat[1:2, :]

    kv_sum_rings = [
        sum_ring(i, lambda slot, i=i: kvpart[i, slot * 128 : slot * 128 + 128, :], rsend, rrecv)
        for i in range(2)
    ]

    def backward(s):
        rows = slice(s * 256, s * 256 + 256)
        values = vrel[rows, :]
        for r in range(4):
            lanes = slice(r * 256, r * 256 + 256)
            grad_probs = nn(values, gtall[:, lanes])
            softmax = sp[rows, lanes] * frow[:, lanes]
            smp[:, lanes] = softmax.astype(BF16)
            dsb[rows, lanes] = (softmax * (grad_probs - drow[:, lanes])).astype(BF16)
        kvpart[0, rows, :] = nn(dsb[rows, :], qall[...]) * SCALE
        kvpart[1, rows, :] = nt(smp[...], gtall[...])

    backward(0)
    kv_sum_rings[0][0](0)
    backward(1)
    kv_sum_rings[1][0](0)
    for copy in (at_copies[1], at_copies[3], at_far[0], at_far[1]):
        copy.wait_recv()
    dwp[...] = nt(at[...], dot2[...])
    for step, _ in dw_rings:
        step(0)
    backward(2)
    backward(3)
    for s in range(1, 4):
        for step, _ in kv_sum_rings + dw_rings:
            step(s)

    dq_sem = sems.take(4)
    dq_copies = []
    for r in (1, 2, 3, 0):
        lanes = slice(r * 256, r * 256 + 256)
        part = nn(kt[...], dsb[:, lanes]) * SCALE
        if r == 0:
            dqown[...] = part
        else:
            k = 4 - r
            dqsend[r] = part.astype(BF16)
            dq_copies.append(
                sems.copy(dqsend.at[r], dqbuf.at[k], dq_sem + k, dq_sem + k, *group_peer(k))
            )
            dq_copies[-1].start()
    pending += dq_copies

    for i, (_, finish) in enumerate(kv_sum_rings):
        kvfin_send[i] = finish().T.astype(BF16)
    fin_send = sems.take(4)
    fin_recv = sems.take(4)
    source = lax.rem(yhi - key_quarter + 4, 4)
    fin_copies = []
    for k in range(4):
        column = lax.rem(m + k, 4)
        fin_copies.append(
            sems.copy(
                kvfin_send.at[:, pl.ds(pl.multiple_of(column * 32, 32), 32), :],
                kvfin.at[source],
                fin_send + k,
                fin_recv + source,
                g * 4 + column,
                key_quarter * 8 + z,
            )
        )
    for k in range(1, 4):
        fin_copies[k].start()
        pending.append(fin_copies[k])

    @pl.when(key_quarter != yhi)
    def _():
        fin_copies[0].start()

    @pl.when(key_quarter == yhi)
    def _():
        kvfin[0] = kvfin_send[:, pl.ds(pl.multiple_of(m * 32, 32), 32), :]

    for i, (_, finish) in enumerate(dw_rings):
        total = finish().astype(BF16)
        for y in range(2):
            dwsend[2 * i + y] = total[y * 80 : y * 80 + 80, :]
    dwf_sem = sems.take(4)
    dwf_copies = []
    for k in range(1, 4):
        dwf_copies.append(
            sems.copy(
                dwsend.at[lax.rem(yhi + k, 4)], dwfin.at[yhi], dwf_sem + k, dwf_sem + k, *y_peer(k)
            )
        )
        dwf_copies[-1].start()
    pending += dwf_copies
    dwfin[yhi] = dwsend[yhi]

    for copy in dq_copies:
        copy.wait_recv()
    query_grad = dqown[...]
    for k in range(1, 4):
        query_grad = query_grad + dqbuf[k].astype(F32)
    query_rows = jnp.concatenate([query_grad[:, :128], query_grad[:, 128:]], axis=0)
    dq_ref[...] = query_rows.T.astype(BF16)

    def fin_wait(s):
        sems.copy(
            kvfin_send.at[:, pl.ds(0, 32), :],
            kvfin.at[s],
            fin_send,
            fin_recv + s,
            *y_peer(1),
        ).wait_recv()

    for s in range(1, 4):
        fin_wait(s)

    @pl.when(key_quarter != yhi)
    def _():
        fin_wait(0)

    for i, out in ((0, dk_ref), (1, dv_ref)):
        total = kvfin[0, i].astype(F32)
        for s in range(1, 4):
            total = total + kvfin[s, i].astype(F32)
        out[...] = total.astype(BF16)

    for copy in dwf_copies:
        copy.wait_recv()
    columns = []
    blocks = [dwfin[q].astype(F32) for q in range(4)]
    for half in range(2):
        for pair in range(2):
            a, c = (
                [
                    blocks[2 * half + i][(pair * 5 + t) * 8 : (pair * 5 + t) * 8 + 8, :]
                    for t in range(5)
                ]
                for i in range(2)
            )
            columns += [
                a[0],
                a[1],
                join(a[2], turn(c[0])),
                join(turn(c[0]), turn(c[1])),
                join(turn(c[1]), turn(c[2])),
                join(turn(a[2]), turn(a[3])),
                join(turn(a[3]), turn(a[4])),
                join(turn(a[4]), c[2]),
                c[3],
                c[4],
            ]
    dw_ref[...] = jnp.concatenate(columns, axis=1).astype(BF16)

    for copy in pending:
        copy.wait_send()

    @pl.when(key_quarter == yhi)
    def _():
        for copy in kv_hop_copies:
            copy.wait_send()

    @pl.when(quarter != yhi)
    def _():
        turn_copy.wait_send()

    @pl.when(key_quarter != yhi)
    def _():
        fin_copies[0].wait_send()

    assert sems.used <= SEM_COUNT, sems.used


def deliver_kernel(*refs):
    count = len(refs) // 2
    for i in range(count):
        refs[count + i][...] = refs[i][...]


def deliver(results):
    vmem = pl.BlockSpec(memory_space=pltpu.VMEM)
    return pl.pallas_call(
        deliver_kernel,
        out_shape=[jax.ShapeDtypeStruct(r.shape, r.dtype) for r in results],
        in_specs=[vmem] * len(results),
        out_specs=[vmem] * len(results),
        compiler_params=pltpu.CompilerParams(vmem_limit_bytes=63 * 1024 * 1024),
    )(*results)


def per_device(block_order, query_states, key_states, value_states, out_weight, out_grad):
    v = pltpu.VMEM
    vmem = pl.BlockSpec(memory_space=pltpu.VMEM)
    scratch = [
        v((8, 5120), BF16),
        v((2, 128, 128), BF16),
        v((8, 2, 128, 128), BF16),
        v((4, 128, 256), BF16),
        v((1024, 128), BF16),
        v((1024, 128), BF16),
        v((1024, 128), BF16),
        v((128, 1024), BF16),
        v((128, 1024), BF16),
        v((4, 80, 128), BF16),
        v((8, 4, 80, 128), BF16),
        v((256, 1280), F32),
        v((320, 128), BF16),
        v((1280, 512), BF16),
        v((1024, 1024), F32),
        v((8, 1024), F32),
        v((1024, 1024), BF16),
        v((1024, 1024), BF16),
        v((1, 1024), F32),
        v((4, 128, 256), BF16),
        v((4, 128, 256), BF16),
        v((4, 8, 256), F32),
        v((4, 8, 256), F32),
        v((256, 512), BF16),
        v((256, 512), F32),
        v((6, 128, 128), BF16),
        v((2, 128, 128), BF16),
        v((4, 128, 128), BF16),
        v((256, 128), BF16),
        v((4, 256, 128), BF16),
        v((8, 256), F32),
        v((4, 8, 256), F32),
        v((128, 1024), BF16),
        v((1, 1024), F32),
        v((1, 1024), F32),
        v((256, 1024), BF16),
        v((2, 1024, 128), F32),
        v((2, 2, 4, 128, 128), BF16),
        v((2, 2, 4, 128, 128), BF16),
        v((2, 128, 128), BF16),
        v((4, 2, 32, 128), BF16),
        v((4, 128, 256), BF16),
        v((4, 128, 256), BF16),
        v((128, 256), F32),
        v((256, 1280), F32),
        v((2, 2, 4, 160, 128), BF16),
        v((2, 2, 4, 160, 128), BF16),
        v((4, 80, 128), BF16),
        v((4, 80, 128), BF16),
        pltpu.SemaphoreType.DMA((SEM_COUNT,)),
        pltpu.SemaphoreType.DMA((SEM_COUNT,)),
        pltpu.SemaphoreType.DMA((5,)),
    ]
    results = pl.pallas_call(
        kernel,
        out_shape=(
            jax.ShapeDtypeStruct((128, 256), BF16),
            jax.ShapeDtypeStruct((128, 256), BF16),
            jax.ShapeDtypeStruct((32, 128), BF16),
            jax.ShapeDtypeStruct((32, 128), BF16),
            jax.ShapeDtypeStruct((8, 5120), BF16),
        ),
        in_specs=[pl.BlockSpec(memory_space=pltpu.SMEM)] + [pl.BlockSpec(memory_space=pltpu.HBM)] * 5,
        out_specs=[vmem] * 5,
        scratch_shapes=scratch,
        compiler_params=pltpu.CompilerParams(
            collective_id=0, has_side_effects=True, vmem_limit_bytes=63 * 1024 * 1024
        ),
        cost_estimate=pl.CostEstimate(
            flops=2_500_000_000, bytes_accessed=1_000_000, transcendentals=1_100_000
        ),
    )(block_order, query_states, key_states, value_states, out_weight, out_grad.T)
    results = deliver(results)
    return results[0], results[1], results[2].T, results[3].T, results[4]


def solution(mesh):
    in_specs = (
        P(),
        P("ctx", "node"),
        P("ctx", None),
        P("ctx", None),
        P(("node", "ctx"), None),
        P("ctx", "node"),
    )
    out_specs = (
        P("ctx", "node"),
        P("ctx", "node"),
        P("ctx", "node"),
        P("ctx", "node"),
        P(("node", "ctx"), None),
    )
    return jax.shard_map(
        per_device, mesh=mesh, in_specs=in_specs, out_specs=out_specs, check_vma=False
    )
```

```python
import functools
import math

import jax
import jax.numpy as jnp
from jax import lax
from jax.experimental import pallas as pl
from jax.experimental.pallas import tpu as pltpu
from jax.sharding import PartitionSpec as P

HD = 128
TOK = 128
NEG = -1e30
SCALE = 1.0 / math.sqrt(HD)
LOG2E = math.log2(math.e)
F32 = jnp.float32
BF16 = jnp.bfloat16
MESH = pl.DeviceIdType.MESH

OFFSET = (4, 5, 3, 6, 2, 7, 1, 0)
RIGHT_SLOT = (5, 3, 1, 0)
LEFT_SLOT = (6, 4, 2, 0)
STEPS = ((4, 3), (3, 4))
RIGHT_SUM = ((0, 2, 4, 6), (2, 4, 6))
LEFT_SUM = ((1, 3, 5), (0, 1, 3, 5))


def nn(a, b):
    return lax.dot_general(a, b, (((1,), (0,)), ((), ())), preferred_element_type=F32)


def nt(a, b):
    return lax.dot_general(a, b, (((1,), (1,)), ((), ())), preferred_element_type=F32)


def fold8(a):
    return a.reshape(a.shape[0] // 8, 8, a.shape[1])


class Sems:
    def __init__(self, send, recv):
        self.send, self.recv, self.used = send, recv, 0

    def take(self, count):
        base = self.used
        self.used += count
        return base

    def copy(self, src, dst, sid, rid, node, ctx):
        return pltpu.make_async_remote_copy(
            src_ref=src,
            dst_ref=dst,
            send_sem=self.send.at[sid],
            recv_sem=self.recv.at[rid],
            device_id={"node": node, "ctx": ctx},
            device_id_type=MESH,
        )


SEM_COUNT = 128


def kernel(
    order_ref, q_ref, k_ref, v_ref, w_ref, og_ref,
    attn_ref, dq_ref, dk_ref, dv_ref, dw_ref,
    wv, kvg, kv, qbuf, qall, krel, vrel, kt, vt,
    wsl, wring, w32, ogt, dot2,
    sp, mx, pb, dsb, mloc,
    osend, obuf, ostat, ostatbuf,
    at, gpart, gpsend, gpbuf, gown, gbuf, gstat, gstatbuf, gtall, frow, drow,
    smp, kvpart, rsend, rrecv, kvfin_send, kvfin,
    dqsend, dqbuf, dqown,
    dwp, wsend, wrecv, dwsend, dwfin,
    send_sem, recv_sem, load_sem,
):
    node = lax.axis_index("node")
    ctx = lax.axis_index("ctx")
    core = lax.rem(node, 2)
    x = lax.rem(node // 2, 4)
    ylo = node // 8
    g = node // 4
    quarter = ylo * 2 + core
    key_quarter = core * 2 + lax.rem(x, 2)
    m = lax.rem(node, 4)
    yhi = ctx // 8
    z = lax.rem(ctx, 8)

    sems = Sems(send_sem, recv_sem)
    pending = []

    def y_peer(k):
        return node, lax.rem(yhi + k, 4) * 8 + z

    def group_peer(k):
        return g * 4 + lax.rem(m + k, 4), ctx

    z_right = (node, yhi * 8 + lax.rem(z + 1, 8))
    z_left = (node, yhi * 8 + lax.rem(z + 7, 8))
    x_right = ((ylo * 4 + lax.rem(x + 1, 4)) * 2 + core, ctx)
    x_left = ((ylo * 4 + lax.rem(x + 3, 4)) * 2 + core, ctx)
    y_flip = (((1 - ylo) * 4 + x) * 2 + core, ctx)
    sibling = (node + 1 - 2 * core, ctx)
    turned = (((yhi // 2) * 4 + x) * 2 + lax.rem(yhi, 2), quarter * 8 + z)

    glane = pl.ds(pl.multiple_of(g * HD, HD), HD)
    loads = [
        pltpu.make_async_copy(og_ref, ogt, load_sem.at[0]),
        pltpu.make_async_copy(w_ref, wv, load_sem.at[1]),
        pltpu.make_async_copy(k_ref.at[:, glane], kvg.at[0], load_sem.at[2]),
        pltpu.make_async_copy(v_ref.at[:, glane], kvg.at[1], load_sem.at[3]),
        pltpu.make_async_copy(q_ref, qbuf.at[0], load_sem.at[4]),
    ]
    for load in loads:
        load.start()

    barrier = pltpu.get_barrier_semaphore()

    def greet(peer):
        pl.semaphore_signal(
            barrier, inc=1, device_id={"node": peer[0], "ctx": peer[1]}, device_id_type=MESH
        )

    for k in range(1, 4):
        greet(y_peer(k))
        greet(group_peer(k))
    for peer in (z_right, z_left, x_right, x_left, y_flip):
        greet(peer)

    @pl.when(quarter != yhi)
    def _():
        greet(turned)

    @pl.when(key_quarter != yhi)
    def _():
        for k in range(1, 4):
            greet((g * 4 + lax.rem(yhi, 2) * 2 + yhi // 2, lax.rem(yhi + k, 4) * 8 + z))

    loads[0].wait()
    low_half = lax.broadcasted_iota(jnp.int32, (8, 128), 1) < 64

    def join(a, b):
        return jnp.where(low_half, a, b)

    def turn(a):
        return pltpu.roll(a, 64, 1)

    pl.semaphore_wait(
        barrier, 11 + jnp.where(quarter != yhi, 1, 0) + jnp.where(key_quarter != yhi, 3, 0)
    )

    def dot_rows(position):
        return pl.ds(pl.multiple_of(position * 320, 64), 320)

    def dot_lanes(position):
        return pl.ds(pl.multiple_of(position * TOK, TOK), TOK)

    turn_sem = sems.take(1)
    turn_copy = sems.copy(
        ogt, dot2.at[dot_rows(x), dot_lanes(yhi)], turn_sem, turn_sem, *turned
    )

    @pl.when(quarter != yhi)
    def _():
        turn_copy.start()

    @pl.when(quarter == yhi)
    def _():
        dot2[dot_rows(x), dot_lanes(yhi)] = ogt[...]

    loads[1].wait()
    w_rows = wv[...].astype(F32)
    for half in range(2):
        even, odd = [], []
        for pair in range(2):
            base = 20 * half + 10 * pair
            w = [w_rows[:, t * 128 : t * 128 + 128] for t in range(base, base + 10)]
            r = {t: turn(w[t]) for t in range(2, 8)}
            shifted = {t: join(r[t], r[t + 1]) for t in range(2, 7)}
            even += [w[0], w[1], join(w[2], shifted[4]), shifted[5], shifted[6]]
            odd += [shifted[2], shifted[3], join(shifted[4], w[7]), w[8], w[9]]
        wsl[2 * half] = jnp.concatenate(even, axis=0).astype(BF16)
        wsl[2 * half + 1] = jnp.concatenate(odd, axis=0).astype(BF16)

    w_sem = sems.take(4)
    w_copies = []
    for k in range(1, 4):
        peer = y_peer(k)
        w_copies.append(
            sems.copy(
                wsl.at[lax.rem(yhi + k, 4)], wring.at[7, yhi], w_sem + k, w_sem + k, *peer
            )
        )
        w_copies[-1].start()
    pending += w_copies
    wring[7, yhi] = wsl[yhi]

    for load in loads[2:]:
        load.wait()

    kv_hop = sems.take(4)
    kv_hop_copies = [
        sems.copy(kvg, kv.at[7], kv_hop + k, kv_hop, *y_peer(k)) for k in range(1, 4)
    ]

    @pl.when(key_quarter == yhi)
    def _():
        for copy in kv_hop_copies:
            copy.start()

    q_sem = sems.take(4)
    q_copies = [
        sems.copy(qbuf.at[0], qbuf.at[k], q_sem + k, q_sem + k, *group_peer(k))
        for k in range(1, 4)
    ]
    for copy in q_copies:
        copy.start()
    pending += q_copies

    def ring(half, view):
        base = sems.take(7)
        ways = []
        for count, slots, peer in zip(STEPS[half], (RIGHT_SLOT, LEFT_SLOT), (z_right, z_left)):
            ways.append(
                [
                    sems.copy(
                        view(7 if s == 0 else slots[s - 1]),
                        view(slots[s]),
                        base + s,
                        base + s,
                        *peer,
                    )
                    for s in range(count)
                ]
            )
            base += count
        return ways

    def ring_step(rings, s):
        for ways in rings:
            for copies in ways:
                if 0 < s <= len(copies):
                    copies[s - 1].wait_recv()
                if s < len(copies):
                    copies[s].start()
                    pending.append(copies[s])

    kv_ring = [ring(i, lambda slot, i=i: kv.at[slot, i]) for i in range(2)]
    w_ring = [ring(i, lambda slot, i=i: wring.at[slot, pl.ds(2 * i, 2)]) for i in range(2)]

    @pl.when(quarter != yhi)
    def _():
        turn_copy.wait_recv()

    other_quarter = (1 - ylo) * 2 + core
    flip_sem = sems.take(1)
    own_block = dot2.at[dot_rows(x), dot_lanes(quarter)]
    flip_block = dot2.at[dot_rows(x), dot_lanes(other_quarter)]
    x_sem = sems.take(6)
    flip_copy = sems.copy(own_block, own_block, flip_sem, flip_sem, *y_flip)
    x_own = [
        sems.copy(own_block, own_block, x_sem, x_sem, *x_right),
        sems.copy(own_block, own_block, x_sem + 1, x_sem + 1, *x_left),
    ]
    x_flip = [
        sems.copy(flip_block, flip_block, x_sem + 2, x_sem + 2, *x_right),
        sems.copy(flip_block, flip_block, x_sem + 3, x_sem + 3, *x_left),
    ]
    for copy in [flip_copy] + x_own:
        copy.start()
        pending.append(copy)

    core_sem = sems.take(8)
    core_copies = []

    def share(row_position, lane_position):
        block = dot2.at[dot_rows(row_position), dot_lanes(lane_position)]
        sem = core_sem + len(core_copies)
        core_copies.append(sems.copy(block, block, sem, sem, *sibling))
        core_copies[-1].start()
        pending.append(core_copies[-1])

    share(x, quarter)

    for copy in w_copies:
        copy.wait_recv()
    ring_step(w_ring, 0)

    @pl.when(key_quarter == yhi)
    def _():
        kv[7] = kvg[...]

    @pl.when(key_quarter != yhi)
    def _():
        sems.copy(kvg, kv.at[7], kv_hop, kv_hop, *y_peer(1)).wait_recv()

    ring_step(kv_ring, 0)

    def unpack_weight(slot):
        first = lax.rem(z + OFFSET[slot], 8) * 8
        for y in range(4):
            block = wring[slot, y].astype(F32)
            rows = pl.ds(pl.multiple_of(first + y * 64, 8), 8)
            for j in range(10):
                w32[rows, j * 128 : j * 128 + 128] = block[j * 8 : j * 8 + 8, :]

    unpack_weight(7)

    for copy in q_copies:
        copy.wait_recv()
    for r in range(4):
        for h in range(2):
            qall[r * 256 + h * 128 : r * 256 + h * 128 + 128, :] = qbuf[
                r, :, h * 128 : h * 128 + 128
            ]

    def place(first_block, dim):
        index = lax.broadcasted_iota(jnp.int32, (TOK, TOK), dim)
        low = order_ref[first_block] * 64 + index
        high = order_ref[first_block + 1] * 64 + (index - 64)
        return jnp.where(index < 64, low, high)

    query_place = place(ctx * 2, 1)
    mx[...] = jnp.full(mx.shape, NEG, F32)

    def score_block(slot):
        block = key_quarter * 8 + lax.rem(z + OFFSET[slot], 8)
        allowed = place(block * 2, 0) <= query_place
        allowed = jnp.concatenate([allowed, allowed], axis=1)
        rows = slice(slot * 128, slot * 128 + 128)
        keys = kv[slot, 0]
        values = kv[slot, 1]
        krel[rows, :] = keys
        vrel[rows, :] = values
        kt[:, rows] = keys.astype(F32).T.astype(BF16)
        vt[:, rows] = values.astype(F32).T.astype(BF16)
        for r in range(4):
            lanes = slice(r * 256, r * 256 + 256)
            scores = nt(keys, qall[lanes, :]) * (SCALE * LOG2E)
            scores = jnp.where(allowed, scores, NEG)
            sp[rows, lanes] = scores
            mx[:, lanes] = jnp.maximum(mx[:, lanes], jnp.max(fold8(scores), axis=0))

    score_block(7)

    flip_copy.wait_recv()
    for copy in x_flip:
        copy.start()
    pending += x_flip
    share(x, other_quarter)
    ring_step(w_ring, 1)
    ring_step(kv_ring, 1)
    score_block(5)
    score_block(6)
    unpack_weight(5)
    unpack_weight(6)

    x_own[0].wait_recv()
    far_own = dot2.at[dot_rows(lax.rem(x + 3, 4)), dot_lanes(quarter)]
    x_far = [sems.copy(far_own, far_own, x_sem + 4, x_sem + 4, *x_right)]
    x_far[0].start()
    x_own[1].wait_recv()
    share(lax.rem(x + 3, 4), quarter)
    share(lax.rem(x + 1, 4), quarter)
    ring_step(w_ring, 2)
    ring_step(kv_ring, 2)
    score_block(3)
    score_block(4)
    unpack_weight(3)
    unpack_weight(4)
    x_flip[1].wait_recv()
    far_flip = dot2.at[dot_rows(lax.rem(x + 1, 4)), dot_lanes(other_quarter)]
    x_far.append(sems.copy(far_flip, far_flip, x_sem + 5, x_sem + 5, *x_left))
    x_far[1].start()
    x_flip[0].wait_recv()
    share(lax.rem(x + 3, 4), other_quarter)
    share(lax.rem(x + 1, 4), other_quarter)
    pending += x_far

    ring_step(w_ring, 3)
    ring_step(kv_ring, 3)
    score_block(1)
    score_block(2)
    unpack_weight(1)
    unpack_weight(2)
    for copy in x_far:
        copy.wait_recv()
    share(lax.rem(x + 2, 4), quarter)
    share(lax.rem(x + 2, 4), other_quarter)

    ring_step(w_ring, 4)
    unpack_weight(0)
    weight = w32[...].astype(BF16)
    for copy in core_copies:
        copy.wait_recv()
    gpart[...] = nn(weight, dot2[...])
    heads = (slice(0, 128), slice(128, 256))
    lanes_of = [dot_lanes(lax.rem(yhi + k, 4)) for k in range(4)]
    my_lanes = lanes_of[0]
    gp_sem = sems.take(4)
    gp_copies = []
    for k in (2, 1, 3):
        gpsend[k] = gpart[:, lanes_of[k]].astype(BF16)
        gp_copies.append(
            sems.copy(gpsend.at[k], gpbuf.at[k], gp_sem + k, gp_sem + k, *y_peer(k))
        )
        gp_copies[-1].start()
    pending += gp_copies
    ring_step(kv_ring, 4)
    score_block(0)

    o_sem = sems.take(8)
    o_copies = []

    def forward(r):
        lanes = slice(r * 256, r * 256 + 256)
        row_max = jnp.maximum(jnp.max(mx[:, lanes], axis=0, keepdims=True), -1e20)

        def body(i, total):
            rows = pl.ds(pl.multiple_of(i * 128, 128), 128)
            weights = jnp.exp2(sp[rows, lanes] - row_max)
            sp[rows, lanes] = weights
            pb[rows, lanes] = weights.astype(BF16)
            return total + jnp.sum(fold8(weights), axis=0)

        total = lax.fori_loop(0, 8, body, jnp.zeros((8, 256), F32))
        row_sum = jnp.sum(total, axis=0, keepdims=True)
        mloc[:, lanes] = row_max
        return row_max, row_sum, nn(vt[...], pb[:, lanes])

    def stat_rows(first, second):
        index = lax.broadcasted_iota(jnp.int32, (8, 256), 0)
        return jnp.where(index == 0, first, second)

    for r in (2, 1, 3):
        row_max, row_sum, part = forward(r)
        osend[r] = part.astype(BF16)
        ostat[r] = stat_rows(row_max, row_sum)
        k = 4 - r
        peer = group_peer(k)
        o_copies.append(sems.copy(osend.at[r], obuf.at[k], o_sem + k, o_sem + k, *peer))
        o_copies.append(
            sems.copy(ostat.at[r], ostatbuf.at[k], o_sem + 4 + k, o_sem + 4 + k, *peer)
        )
        o_copies[-2].start()
        o_copies[-1].start()
    pending += o_copies
    own_max, own_sum, own_part = forward(0)

    for copy in gp_copies:
        copy.wait_recv()
    grad = gpart[:, my_lanes]
    for k in range(1, 4):
        grad = grad + gpbuf[k].astype(F32)
    grad_bf = grad.astype(BF16)
    gown[...] = grad_bf
    g_sem = sems.take(8)
    g_copies = []
    for k in range(1, 4):
        g_copies.append(sems.copy(gown, gbuf.at[k], g_sem + k, g_sem + k, *group_peer(k)))
        g_copies[-1].start()

    for copy in o_copies:
        copy.wait_recv()
    maxes = [own_max] + [ostatbuf[k, 0:1, :] for k in range(1, 4)]
    sums = [own_sum] + [ostatbuf[k, 1:2, :] for k in range(1, 4)]
    parts = [own_part] + [obuf[k].astype(F32) for k in range(1, 4)]
    top = functools.reduce(jnp.maximum, maxes)
    factors = [jnp.exp2(value - top) for value in maxes]
    total = sum(f * s for f, s in zip(factors, sums))
    attention = sum(f * p for f, p in zip(factors, parts)) / total
    lse = top + jnp.log2(total)
    attention_rows = jnp.concatenate([attention[:, :128], attention[:, 128:]], axis=0)
    attention_bf = attention_rows.astype(BF16)
    at[:, my_lanes] = attention_bf
    at_sem = sems.take(6)
    at_copies = []
    for way, k in ((0, 1), (1, 3)):
        for i, head in enumerate((way, 1 - way)):
            mine = at.at[heads[head], my_lanes]
            sem = at_sem + way * 2 + i
            at_copies.append(sems.copy(mine, mine, sem, sem, *y_peer(k)))
            at_copies[-1].start()
    pending += at_copies
    products = grad_bf.astype(F32) * attention_bf.astype(F32)
    row_dot = jnp.concatenate(
        [
            jnp.sum(products[:128], axis=0, keepdims=True),
            jnp.sum(products[128:], axis=0, keepdims=True),
        ],
        axis=1,
    )
    own_stat = stat_rows(lse, row_dot)
    gstat[...] = own_stat
    for k in range(1, 4):
        g_copies.append(
            sems.copy(gstat, gstatbuf.at[k], g_sem + 4 + k, g_sem + 4 + k, *group_peer(k))
        )
        g_copies[-1].start()
    pending += g_copies

    attn_ref[...] = attention_rows.T.astype(BF16)
    at_far = []
    for way, k in ((0, 1), (1, 3)):
        at_copies[2 * way].wait_recv()
        passed = at.at[heads[way], lanes_of[4 - k]]
        at_far.append(sems.copy(passed, passed, at_sem + 4 + way, at_sem + 4 + way, *y_peer(k)))
        at_far[way].start()
    pending += at_far

    def weight_block(slot, part):
        first = lax.rem(z + OFFSET[slot], 8) * 8
        slabs = []
        for y in (2 * part, 2 * part + 1):
            rows = pl.ds(pl.multiple_of(first + y * 64, 8), 8)
            for j in range(10):
                slabs.append(dwp[rows, j * 128 : j * 128 + 128])
        return jnp.concatenate(slabs, axis=0)

    def sum_ring(half, block, sends, recvs):
        base = sems.take(7)
        ways = []
        for way, (slots, peer) in enumerate(((RIGHT_SUM, z_right), (LEFT_SUM, z_left))):
            slots = slots[half]
            ways.append(
                (
                    way,
                    slots,
                    [
                        sems.copy(
                            sends.at[half, way, s],
                            recvs.at[half, way, s],
                            base + s,
                            base + s,
                            *peer,
                        )
                        for s in range(len(slots))
                    ],
                )
            )
            base += len(slots)

        def step(s):
            for way, slots, copies in ways:
                if s < len(slots):
                    value = block(slots[s])
                    if s > 0:
                        copies[s - 1].wait_recv()
                        value = value + recvs[half, way, s - 1].astype(F32)
                    sends[half, way, s] = value.astype(BF16)
                    copies[s].start()
                    pending.append(copies[s])

        def finish():
            total = block(7)
            for way, slots, copies in ways:
                copies[-1].wait_recv()
                total = total + recvs[half, way, len(slots) - 1].astype(F32)
            return total

        return step, finish

    dw_rings = [
        sum_ring(i, lambda slot, i=i: weight_block(slot, i), wsend, wrecv) for i in range(2)
    ]

    for copy in g_copies:
        copy.wait_recv()
    for r in range(4):
        block = gown[...] if r == 0 else gbuf[r]
        for h in range(2):
            gtall[:, r * 256 + h * 128 : r * 256 + h * 128 + 128] = block[
                h * 128 : h * 128 + 128, :
            ]
        stat = own_stat if r == 0 else gstatbuf[r]
        lanes = slice(r * 256, r * 256 + 256)
        frow[:, lanes] = jnp.exp2(mloc[:, lanes] - stat[0:1, :])
        drow[:, lanes] = stat[1:2, :]

    kv_sum_rings = [
        sum_ring(i, lambda slot, i=i: kvpart[i, slot * 128 : slot * 128 + 128, :], rsend, rrecv)
        for i in range(2)
    ]

    def backward(s):
        rows = slice(s * 256, s * 256 + 256)
        values = vrel[rows, :]
        for r in range(4):
            lanes = slice(r * 256, r * 256 + 256)
            grad_probs = nn(values, gtall[:, lanes])
            softmax = sp[rows, lanes] * frow[:, lanes]
            smp[:, lanes] = softmax.astype(BF16)
            dsb[rows, lanes] = (softmax * (grad_probs - drow[:, lanes])).astype(BF16)
        kvpart[0, rows, :] = nn(dsb[rows, :], qall[...]) * SCALE
        kvpart[1, rows, :] = nt(smp[...], gtall[...])

    backward(0)
    kv_sum_rings[0][0](0)
    backward(1)
    kv_sum_rings[1][0](0)
    for copy in (at_copies[1], at_copies[3], at_far[0], at_far[1]):
        copy.wait_recv()
    dwp[...] = nt(at[...], dot2[...])
    for step, _ in dw_rings:
        step(0)
    backward(2)
    backward(3)
    for s in range(1, 4):
        for step, _ in kv_sum_rings + dw_rings:
            step(s)

    dq_sem = sems.take(4)
    dq_copies = []
    for r in (1, 2, 3, 0):
        lanes = slice(r * 256, r * 256 + 256)
        part = nn(kt[...], dsb[:, lanes]) * SCALE
        if r == 0:
            dqown[...] = part
        else:
            k = 4 - r
            dqsend[r] = part.astype(BF16)
            dq_copies.append(
                sems.copy(dqsend.at[r], dqbuf.at[k], dq_sem + k, dq_sem + k, *group_peer(k))
            )
            dq_copies[-1].start()
    pending += dq_copies

    for i, (_, finish) in enumerate(kv_sum_rings):
        kvfin_send[i] = finish().T.astype(BF16)
    fin_send = sems.take(4)
    fin_recv = sems.take(4)
    source = lax.rem(yhi - key_quarter + 4, 4)
    fin_copies = []
    for k in range(4):
        column = lax.rem(m + k, 4)
        fin_copies.append(
            sems.copy(
                kvfin_send.at[:, pl.ds(pl.multiple_of(column * 32, 32), 32), :],
                kvfin.at[source],
                fin_send + k,
                fin_recv + source,
                g * 4 + column,
                key_quarter * 8 + z,
            )
        )
    for k in range(1, 4):
        fin_copies[k].start()
        pending.append(fin_copies[k])

    @pl.when(key_quarter != yhi)
    def _():
        fin_copies[0].start()

    @pl.when(key_quarter == yhi)
    def _():
        kvfin[0] = kvfin_send[:, pl.ds(pl.multiple_of(m * 32, 32), 32), :]

    for i, (_, finish) in enumerate(dw_rings):
        total = finish().astype(BF16)
        for y in range(2):
            dwsend[2 * i + y] = total[y * 80 : y * 80 + 80, :]
    dwf_sem = sems.take(4)
    dwf_copies = []
    for k in range(1, 4):
        dwf_copies.append(
            sems.copy(
                dwsend.at[lax.rem(yhi + k, 4)], dwfin.at[yhi], dwf_sem + k, dwf_sem + k, *y_peer(k)
            )
        )
        dwf_copies[-1].start()
    pending += dwf_copies
    dwfin[yhi] = dwsend[yhi]

    for copy in dq_copies:
        copy.wait_recv()
    query_grad = dqown[...]
    for k in range(1, 4):
        query_grad = query_grad + dqbuf[k].astype(F32)
    query_rows = jnp.concatenate([query_grad[:, :128], query_grad[:, 128:]], axis=0)
    dq_ref[...] = query_rows.T.astype(BF16)

    def fin_wait(s):
        sems.copy(
            kvfin_send.at[:, pl.ds(0, 32), :],
            kvfin.at[s],
            fin_send,
            fin_recv + s,
            *y_peer(1),
        ).wait_recv()

    for s in range(1, 4):
        fin_wait(s)

    @pl.when(key_quarter != yhi)
    def _():
        fin_wait(0)

    for i, out in ((0, dk_ref), (1, dv_ref)):
        total = kvfin[0, i].astype(F32)
        for s in range(1, 4):
            total = total + kvfin[s, i].astype(F32)
        out[...] = total.astype(BF16)

    for copy in dwf_copies:
        copy.wait_recv()
    columns = []
    blocks = [dwfin[q].astype(F32) for q in range(4)]
    for half in range(2):
        for pair in range(2):
            a, c = (
                [
                    blocks[2 * half + i][(pair * 5 + t) * 8 : (pair * 5 + t) * 8 + 8, :]
                    for t in range(5)
                ]
                for i in range(2)
            )
            columns += [
                a[0],
                a[1],
                join(a[2], turn(c[0])),
                join(turn(c[0]), turn(c[1])),
                join(turn(c[1]), turn(c[2])),
                join(turn(a[2]), turn(a[3])),
                join(turn(a[3]), turn(a[4])),
                join(turn(a[4]), c[2]),
                c[3],
                c[4],
            ]
    dw_ref[...] = jnp.concatenate(columns, axis=1).astype(BF16)

    for copy in pending:
        copy.wait_send()

    @pl.when(key_quarter == yhi)
    def _():
        for copy in kv_hop_copies:
            copy.wait_send()

    @pl.when(quarter != yhi)
    def _():
        turn_copy.wait_send()

    @pl.when(key_quarter != yhi)
    def _():
        fin_copies[0].wait_send()

    assert sems.used <= SEM_COUNT, sems.used


def deliver_kernel(*refs):
    count = len(refs) // 2
    for i in range(count):
        refs[count + i][...] = refs[i][...]


def deliver(results):
    vmem = pl.BlockSpec(memory_space=pltpu.VMEM)
    return pl.pallas_call(
        deliver_kernel,
        out_shape=[jax.ShapeDtypeStruct(r.shape, r.dtype) for r in results],
        in_specs=[vmem] * len(results),
        out_specs=[vmem] * len(results),
        compiler_params=pltpu.CompilerParams(vmem_limit_bytes=63 * 1024 * 1024),
    )(*results)


def per_device(block_order, query_states, key_states, value_states, out_weight, out_grad):
    v = pltpu.VMEM
    vmem = pl.BlockSpec(memory_space=pltpu.VMEM)
    scratch = [
        v((8, 5120), BF16),
        v((2, 128, 128), BF16),
        v((8, 2, 128, 128), BF16),
        v((4, 128, 256), BF16),
        v((1024, 128), BF16),
        v((1024, 128), BF16),
        v((1024, 128), BF16),
        v((128, 1024), BF16),
        v((128, 1024), BF16),
        v((4, 80, 128), BF16),
        v((8, 4, 80, 128), BF16),
        v((256, 1280), F32),
        v((320, 128), BF16),
        v((1280, 512), BF16),
        v((1024, 1024), F32),
        v((8, 1024), F32),
        v((1024, 1024), BF16),
        v((1024, 1024), BF16),
        v((1, 1024), F32),
        v((4, 128, 256), BF16),
        v((4, 128, 256), BF16),
        v((4, 8, 256), F32),
        v((4, 8, 256), F32),
        v((256, 512), BF16),
        v((256, 512), F32),
        v((4, 256, 128), BF16),
        v((4, 256, 128), BF16),
        v((256, 128), BF16),
        v((4, 256, 128), BF16),
        v((8, 256), F32),
        v((4, 8, 256), F32),
        v((128, 1024), BF16),
        v((1, 1024), F32),
        v((1, 1024), F32),
        v((256, 1024), BF16),
        v((2, 1024, 128), F32),
        v((2, 2, 4, 128, 128), BF16),
        v((2, 2, 4, 128, 128), BF16),
        v((2, 128, 128), BF16),
        v((4, 2, 32, 128), BF16),
        v((4, 128, 256), BF16),
        v((4, 128, 256), BF16),
        v((128, 256), F32),
        v((256, 1280), F32),
        v((2, 2, 4, 160, 128), BF16),
        v((2, 2, 4, 160, 128), BF16),
        v((4, 80, 128), BF16),
        v((4, 80, 128), BF16),
        pltpu.SemaphoreType.DMA((SEM_COUNT,)),
        pltpu.SemaphoreType.DMA((SEM_COUNT,)),
        pltpu.SemaphoreType.DMA((5,)),
    ]
    results = pl.pallas_call(
        kernel,
        out_shape=(
            jax.ShapeDtypeStruct((128, 256), BF16),
            jax.ShapeDtypeStruct((128, 256), BF16),
            jax.ShapeDtypeStruct((32, 128), BF16),
            jax.ShapeDtypeStruct((32, 128), BF16),
            jax.ShapeDtypeStruct((8, 5120), BF16),
        ),
        in_specs=[pl.BlockSpec(memory_space=pltpu.SMEM)] + [pl.BlockSpec(memory_space=pltpu.HBM)] * 5,
        out_specs=[vmem] * 5,
        scratch_shapes=scratch,
        compiler_params=pltpu.CompilerParams(
            collective_id=0, has_side_effects=True, vmem_limit_bytes=63 * 1024 * 1024
        ),
        cost_estimate=pl.CostEstimate(
            flops=2_500_000_000, bytes_accessed=1_000_000, transcendentals=1_100_000
        ),
    )(block_order, query_states, key_states, value_states, out_weight, out_grad.T)
    results = deliver(results)
    return results[0], results[1], results[2].T, results[3].T, results[4]


def solution(mesh):
    in_specs = (
        P(),
        P("ctx", "node"),
        P("ctx", None),
        P("ctx", None),
        P(("node", "ctx"), None),
        P("ctx", "node"),
    )
    out_specs = (
        P("ctx", "node"),
        P("ctx", "node"),
        P("ctx", "node"),
        P("ctx", "node"),
        P(("node", "ctx"), None),
    )
    return jax.shard_map(
        per_device, mesh=mesh, in_specs=in_specs, out_specs=out_specs, check_vma=False
    )
```

```python
import functools
import math

import jax
import jax.numpy as jnp
from jax import lax
from jax.experimental import pallas as pl
from jax.experimental.pallas import tpu as pltpu
from jax.sharding import PartitionSpec as P

HD = 128
TOK = 128
NEG = -1e30
SCALE = 1.0 / math.sqrt(HD)
LOG2E = math.log2(math.e)
F32 = jnp.float32
BF16 = jnp.bfloat16
MESH = pl.DeviceIdType.MESH

OFFSET = (4, 5, 3, 6, 2, 7, 1, 0)
RIGHT_SLOT = (5, 3, 1, 0)
LEFT_SLOT = (6, 4, 2, 0)
STEPS = ((4, 3), (3, 4))
RIGHT_SUM = ((0, 2, 4, 6), (2, 4, 6))
LEFT_SUM = ((1, 3, 5), (0, 1, 3, 5))


def nn(a, b):
    return lax.dot_general(a, b, (((1,), (0,)), ((), ())), preferred_element_type=F32)


def nt(a, b):
    return lax.dot_general(a, b, (((1,), (1,)), ((), ())), preferred_element_type=F32)


def fold8(a):
    return a.reshape(a.shape[0] // 8, 8, a.shape[1])


class Sems:
    def __init__(self, send, recv):
        self.send, self.recv, self.used = send, recv, 0

    def take(self, count):
        base = self.used
        self.used += count
        return base

    def copy(self, src, dst, sid, rid, node, ctx):
        return pltpu.make_async_remote_copy(
            src_ref=src,
            dst_ref=dst,
            send_sem=self.send.at[sid],
            recv_sem=self.recv.at[rid],
            device_id={"node": node, "ctx": ctx},
            device_id_type=MESH,
        )


SEM_COUNT = 128


def kernel(
    order_ref, q_ref, k_ref, v_ref, w_ref, og_ref,
    attn_ref, dq_ref, dk_ref, dv_ref, dw_ref,
    wv, kvg, kv, qbuf, qall, krel, vrel, kt, vt,
    wsl, wring, w32, ogt, dot2,
    sp, mx, pb, dsb, mloc,
    osend, obuf, ostat, ostatbuf,
    at, gpart, gpsend, gpbuf, gown, gbuf, gstat, gstatbuf, gtall, frow, drow,
    smp, kvpart, rsend, rrecv, kvfin_send, kvfin,
    dqsend, dqbuf, dqown,
    dwp, wsend, wrecv, dwsend, dwfin,
    send_sem, recv_sem, load_sem,
):
    node = lax.axis_index("node")
    ctx = lax.axis_index("ctx")
    core = lax.rem(node, 2)
    x = lax.rem(node // 2, 4)
    ylo = node // 8
    g = node // 4
    quarter = ylo * 2 + core
    key_quarter = core * 2 + lax.rem(x, 2)
    m = lax.rem(node, 4)
    yhi = ctx // 8
    z = lax.rem(ctx, 8)

    sems = Sems(send_sem, recv_sem)
    pending = []

    def y_peer(k):
        return node, lax.rem(yhi + k, 4) * 8 + z

    def group_peer(k):
        return g * 4 + lax.rem(m + k, 4), ctx

    z_right = (node, yhi * 8 + lax.rem(z + 1, 8))
    z_left = (node, yhi * 8 + lax.rem(z + 7, 8))
    x_right = ((ylo * 4 + lax.rem(x + 1, 4)) * 2 + core, ctx)
    x_left = ((ylo * 4 + lax.rem(x + 3, 4)) * 2 + core, ctx)
    x_outer = ((ylo * 4 + lax.rem(x + 3 - 2 * lax.rem(x, 2), 4)) * 2 + core, ctx)
    y_flip = (((1 - ylo) * 4 + x) * 2 + core, ctx)
    sibling = (node + 1 - 2 * core, ctx)
    turned = (((yhi // 2) * 4 + x) * 2 + lax.rem(yhi, 2), quarter * 8 + z)

    glane = pl.ds(pl.multiple_of(g * HD, HD), HD)
    loads = [
        pltpu.make_async_copy(og_ref, ogt, load_sem.at[0]),
        pltpu.make_async_copy(w_ref, wv, load_sem.at[1]),
        pltpu.make_async_copy(k_ref.at[:, glane], kvg.at[0], load_sem.at[2]),
        pltpu.make_async_copy(v_ref.at[:, glane], kvg.at[1], load_sem.at[3]),
        pltpu.make_async_copy(q_ref, qbuf.at[0], load_sem.at[4]),
    ]
    for load in loads:
        load.start()

    barrier = pltpu.get_barrier_semaphore()

    def greet(peer):
        pl.semaphore_signal(
            barrier, inc=1, device_id={"node": peer[0], "ctx": peer[1]}, device_id_type=MESH
        )

    for k in range(1, 4):
        greet(y_peer(k))
        greet(group_peer(k))
    for peer in (z_right, z_left, x_outer, y_flip):
        greet(peer)

    @pl.when(quarter != yhi)
    def _():
        greet(turned)

    @pl.when(key_quarter != yhi)
    def _():
        for k in range(1, 4):
            greet((g * 4 + lax.rem(yhi, 2) * 2 + yhi // 2, lax.rem(yhi + k, 4) * 8 + z))

    loads[0].wait()
    low_half = lax.broadcasted_iota(jnp.int32, (8, 128), 1) < 64

    def join(a, b):
        return jnp.where(low_half, a, b)

    def turn(a):
        return pltpu.roll(a, 64, 1)

    pl.semaphore_wait(
        barrier, 10 + jnp.where(quarter != yhi, 1, 0) + jnp.where(key_quarter != yhi, 3, 0)
    )

    def dot_rows(position):
        return pl.ds(pl.multiple_of(position * 320, 64), 320)

    def dot_lanes(position):
        return pl.ds(pl.multiple_of(position * TOK, TOK), TOK)

    turn_sem = sems.take(1)
    turn_copy = sems.copy(
        ogt, dot2.at[dot_rows(x), dot_lanes(yhi)], turn_sem, turn_sem, *turned
    )

    @pl.when(quarter != yhi)
    def _():
        turn_copy.start()

    @pl.when(quarter == yhi)
    def _():
        dot2[dot_rows(x), dot_lanes(yhi)] = ogt[...]

    loads[1].wait()
    w_rows = wv[...].astype(F32)
    for half in range(2):
        even, odd = [], []
        for pair in range(2):
            base = 20 * half + 10 * pair
            w = [w_rows[:, t * 128 : t * 128 + 128] for t in range(base, base + 10)]
            r = {t: turn(w[t]) for t in range(2, 8)}
            shifted = {t: join(r[t], r[t + 1]) for t in range(2, 7)}
            even += [w[0], w[1], join(w[2], shifted[4]), shifted[5], shifted[6]]
            odd += [shifted[2], shifted[3], join(shifted[4], w[7]), w[8], w[9]]
        wsl[2 * half] = jnp.concatenate(even, axis=0).astype(BF16)
        wsl[2 * half + 1] = jnp.concatenate(odd, axis=0).astype(BF16)

    w_sem = sems.take(4)
    w_copies = []
    for k in range(1, 4):
        peer = y_peer(k)
        w_copies.append(
            sems.copy(
                wsl.at[lax.rem(yhi + k, 4)], wring.at[7, yhi], w_sem + k, w_sem + k, *peer
            )
        )
        w_copies[-1].start()
    pending += w_copies
    wring[7, yhi] = wsl[yhi]

    for load in loads[2:]:
        load.wait()

    kv_hop = sems.take(4)
    kv_hop_copies = [
        sems.copy(kvg, kv.at[7], kv_hop + k, kv_hop, *y_peer(k)) for k in range(1, 4)
    ]

    @pl.when(key_quarter == yhi)
    def _():
        for copy in kv_hop_copies:
            copy.start()

    q_sem = sems.take(4)
    q_copies = [
        sems.copy(qbuf.at[0], qbuf.at[k], q_sem + k, q_sem + k, *group_peer(k))
        for k in range(1, 4)
    ]
    for copy in q_copies:
        copy.start()
    pending += q_copies

    def ring(half, view):
        base = sems.take(7)
        ways = []
        for count, slots, peer in zip(STEPS[half], (RIGHT_SLOT, LEFT_SLOT), (z_right, z_left)):
            ways.append(
                [
                    sems.copy(
                        view(7 if s == 0 else slots[s - 1]),
                        view(slots[s]),
                        base + s,
                        base + s,
                        *peer,
                    )
                    for s in range(count)
                ]
            )
            base += count
        return ways

    def ring_step(rings, s):
        for ways in rings:
            for copies in ways:
                if 0 < s <= len(copies):
                    copies[s - 1].wait_recv()
                if s < len(copies):
                    copies[s].start()
                    pending.append(copies[s])

    kv_ring = [ring(i, lambda slot, i=i: kv.at[slot, i]) for i in range(2)]
    w_ring = [ring(i, lambda slot, i=i: wring.at[slot, pl.ds(2 * i, 2)]) for i in range(2)]

    @pl.when(quarter != yhi)
    def _():
        turn_copy.wait_recv()

    other_quarter = (1 - ylo) * 2 + core
    flip_sem = sems.take(1)
    own_block = dot2.at[dot_rows(x), dot_lanes(quarter)]
    flip_block = dot2.at[dot_rows(x), dot_lanes(other_quarter)]
    x_sem = sems.take(6)
    flip_copy = sems.copy(own_block, own_block, flip_sem, flip_sem, *y_flip)
    x_own = [
        sems.copy(own_block, own_block, x_sem, x_sem, *x_right),
        sems.copy(own_block, own_block, x_sem + 1, x_sem + 1, *x_left),
    ]
    x_flip = [
        sems.copy(flip_block, flip_block, x_sem + 2, x_sem + 2, *x_right),
        sems.copy(flip_block, flip_block, x_sem + 3, x_sem + 3, *x_left),
    ]
    for copy in [flip_copy] + x_own:
        copy.start()
        pending.append(copy)

    core_sem = sems.take(8)
    core_copies = []

    def share(row_position, lane_position):
        block = dot2.at[dot_rows(row_position), dot_lanes(lane_position)]
        sem = core_sem + len(core_copies)
        core_copies.append(sems.copy(block, block, sem, sem, *sibling))
        core_copies[-1].start()
        pending.append(core_copies[-1])

    share(x, quarter)

    for copy in w_copies:
        copy.wait_recv()
    ring_step(w_ring, 0)

    @pl.when(key_quarter == yhi)
    def _():
        kv[7] = kvg[...]

    @pl.when(key_quarter != yhi)
    def _():
        sems.copy(kvg, kv.at[7], kv_hop, kv_hop, *y_peer(1)).wait_recv()

    ring_step(kv_ring, 0)

    def unpack_weight(slot):
        first = lax.rem(z + OFFSET[slot], 8) * 8
        for y in range(4):
            block = wring[slot, y].astype(F32)
            rows = pl.ds(pl.multiple_of(first + y * 64, 8), 8)
            for j in range(10):
                w32[rows, j * 128 : j * 128 + 128] = block[j * 8 : j * 8 + 8, :]

    unpack_weight(7)

    for copy in q_copies:
        copy.wait_recv()
    for r in range(4):
        for h in range(2):
            qall[r * 256 + h * 128 : r * 256 + h * 128 + 128, :] = qbuf[
                r, :, h * 128 : h * 128 + 128
            ]

    def place(first_block, dim):
        index = lax.broadcasted_iota(jnp.int32, (TOK, TOK), dim)
        low = order_ref[first_block] * 64 + index
        high = order_ref[first_block + 1] * 64 + (index - 64)
        return jnp.where(index < 64, low, high)

    query_place = place(ctx * 2, 1)
    mx[...] = jnp.full(mx.shape, NEG, F32)

    def score_block(slot):
        block = key_quarter * 8 + lax.rem(z + OFFSET[slot], 8)
        allowed = place(block * 2, 0) <= query_place
        allowed = jnp.concatenate([allowed, allowed], axis=1)
        rows = slice(slot * 128, slot * 128 + 128)
        keys = kv[slot, 0]
        values = kv[slot, 1]
        krel[rows, :] = keys
        vrel[rows, :] = values
        kt[:, rows] = keys.astype(F32).T.astype(BF16)
        vt[:, rows] = values.astype(F32).T.astype(BF16)
        for r in range(4):
            lanes = slice(r * 256, r * 256 + 256)
            scores = nt(keys, qall[lanes, :]) * (SCALE * LOG2E)
            scores = jnp.where(allowed, scores, NEG)
            sp[rows, lanes] = scores
            mx[:, lanes] = jnp.maximum(mx[:, lanes], jnp.max(fold8(scores), axis=0))

    score_block(7)

    flip_copy.wait_recv()
    for copy in x_flip:
        copy.start()
    pending += x_flip
    share(x, other_quarter)
    ring_step(w_ring, 1)
    ring_step(kv_ring, 1)
    score_block(5)
    score_block(6)
    unpack_weight(5)
    unpack_weight(6)

    x_own[0].wait_recv()
    far_own = dot2.at[dot_rows(lax.rem(x + 3, 4)), dot_lanes(quarter)]
    x_far = [sems.copy(far_own, far_own, x_sem + 4, x_sem + 4, *x_right)]
    x_far[0].start()
    x_own[1].wait_recv()
    share(lax.rem(x + 3, 4), quarter)
    share(lax.rem(x + 1, 4), quarter)
    ring_step(w_ring, 2)
    ring_step(kv_ring, 2)
    score_block(3)
    score_block(4)
    unpack_weight(3)
    unpack_weight(4)
    x_flip[1].wait_recv()
    far_flip = dot2.at[dot_rows(lax.rem(x + 1, 4)), dot_lanes(other_quarter)]
    x_far.append(sems.copy(far_flip, far_flip, x_sem + 5, x_sem + 5, *x_left))
    x_far[1].start()
    x_flip[0].wait_recv()
    share(lax.rem(x + 3, 4), other_quarter)
    share(lax.rem(x + 1, 4), other_quarter)
    pending += x_far

    ring_step(w_ring, 3)
    ring_step(kv_ring, 3)
    score_block(1)
    score_block(2)
    unpack_weight(1)
    unpack_weight(2)
    for copy in x_far:
        copy.wait_recv()
    share(lax.rem(x + 2, 4), quarter)
    share(lax.rem(x + 2, 4), other_quarter)

    ring_step(w_ring, 4)
    unpack_weight(0)
    weight = w32[...].astype(BF16)
    for copy in core_copies:
        copy.wait_recv()
    gpart[...] = nn(weight, dot2[...])
    heads = (slice(0, 128), slice(128, 256))
    lanes_of = [dot_lanes(lax.rem(yhi + k, 4)) for k in range(4)]
    my_lanes = lanes_of[0]
    gp_sem = sems.take(4)
    gp_copies = []
    for k in (2, 1, 3):
        gpsend[k] = gpart[:, lanes_of[k]].astype(BF16)
        gp_copies.append(
            sems.copy(gpsend.at[k], gpbuf.at[k], gp_sem + k, gp_sem + k, *y_peer(k))
        )
        gp_copies[-1].start()
    pending += gp_copies
    ring_step(kv_ring, 4)
    score_block(0)

    o_sem = sems.take(8)
    o_copies = []

    def forward(r):
        lanes = slice(r * 256, r * 256 + 256)
        row_max = jnp.maximum(jnp.max(mx[:, lanes], axis=0, keepdims=True), -1e20)

        def body(i, total):
            rows = pl.ds(pl.multiple_of(i * 128, 128), 128)
            weights = jnp.exp2(sp[rows, lanes] - row_max)
            sp[rows, lanes] = weights
            pb[rows, lanes] = weights.astype(BF16)
            return total + jnp.sum(fold8(weights), axis=0)

        total = lax.fori_loop(0, 8, body, jnp.zeros((8, 256), F32))
        row_sum = jnp.sum(total, axis=0, keepdims=True)
        mloc[:, lanes] = row_max
        return row_max, row_sum, nn(vt[...], pb[:, lanes])

    def stat_rows(first, second):
        index = lax.broadcasted_iota(jnp.int32, (8, 256), 0)
        return jnp.where(index == 0, first, second)

    for r in (2, 1, 3):
        row_max, row_sum, part = forward(r)
        osend[r] = part.astype(BF16)
        ostat[r] = stat_rows(row_max, row_sum)
        k = 4 - r
        peer = group_peer(k)
        o_copies.append(sems.copy(osend.at[r], obuf.at[k], o_sem + k, o_sem + k, *peer))
        o_copies.append(
            sems.copy(ostat.at[r], ostatbuf.at[k], o_sem + 4 + k, o_sem + 4 + k, *peer)
        )
        o_copies[-2].start()
        o_copies[-1].start()
    pending += o_copies
    own_max, own_sum, own_part = forward(0)

    for copy in gp_copies:
        copy.wait_recv()
    grad = gpart[:, my_lanes]
    for k in range(1, 4):
        grad = grad + gpbuf[k].astype(F32)
    grad_bf = grad.astype(BF16)
    gown[...] = grad_bf
    g_sem = sems.take(8)
    g_copies = []
    for k in range(1, 4):
        g_copies.append(sems.copy(gown, gbuf.at[k], g_sem + k, g_sem + k, *group_peer(k)))
        g_copies[-1].start()

    for copy in o_copies:
        copy.wait_recv()
    maxes = [own_max] + [ostatbuf[k, 0:1, :] for k in range(1, 4)]
    sums = [own_sum] + [ostatbuf[k, 1:2, :] for k in range(1, 4)]
    parts = [own_part] + [obuf[k].astype(F32) for k in range(1, 4)]
    top = functools.reduce(jnp.maximum, maxes)
    factors = [jnp.exp2(value - top) for value in maxes]
    total = sum(f * s for f, s in zip(factors, sums))
    attention = sum(f * p for f, p in zip(factors, parts)) / total
    lse = top + jnp.log2(total)
    attention_rows = jnp.concatenate([attention[:, :128], attention[:, 128:]], axis=0)
    attention_bf = attention_rows.astype(BF16)
    at[:, my_lanes] = attention_bf
    at_sem = sems.take(6)
    at_copies = []
    for way, k in ((0, 1), (1, 3)):
        for i, head in enumerate((way, 1 - way)):
            mine = at.at[heads[head], my_lanes]
            sem = at_sem + way * 2 + i
            at_copies.append(sems.copy(mine, mine, sem, sem, *y_peer(k)))
            at_copies[-1].start()
    pending += at_copies
    products = grad_bf.astype(F32) * attention_bf.astype(F32)
    row_dot = jnp.concatenate(
        [
            jnp.sum(products[:128], axis=0, keepdims=True),
            jnp.sum(products[128:], axis=0, keepdims=True),
        ],
        axis=1,
    )
    own_stat = stat_rows(lse, row_dot)
    gstat[...] = own_stat
    for k in range(1, 4):
        g_copies.append(
            sems.copy(gstat, gstatbuf.at[k], g_sem + 4 + k, g_sem + 4 + k, *group_peer(k))
        )
        g_copies[-1].start()
    pending += g_copies

    attn_ref[...] = attention_rows.T.astype(BF16)
    at_far = []
    for way, k in ((0, 1), (1, 3)):
        at_copies[2 * way].wait_recv()
        passed = at.at[heads[way], lanes_of[4 - k]]
        at_far.append(sems.copy(passed, passed, at_sem + 4 + way, at_sem + 4 + way, *y_peer(k)))
        at_far[way].start()
    pending += at_far

    def weight_block(slot, part):
        first = lax.rem(z + OFFSET[slot], 8) * 8
        slabs = []
        for y in (2 * part, 2 * part + 1):
            rows = pl.ds(pl.multiple_of(first + y * 64, 8), 8)
            for j in range(10):
                slabs.append(dwp[rows, j * 128 : j * 128 + 128])
        return jnp.concatenate(slabs, axis=0)

    def sum_ring(half, block, sends, recvs):
        base = sems.take(7)
        ways = []
        for way, (slots, peer) in enumerate(((RIGHT_SUM, z_right), (LEFT_SUM, z_left))):
            slots = slots[half]
            ways.append(
                (
                    way,
                    slots,
                    [
                        sems.copy(
                            sends.at[half, way, s],
                            recvs.at[half, way, s],
                            base + s,
                            base + s,
                            *peer,
                        )
                        for s in range(len(slots))
                    ],
                )
            )
            base += len(slots)

        def step(s):
            for way, slots, copies in ways:
                if s < len(slots):
                    value = block(slots[s])
                    if s > 0:
                        copies[s - 1].wait_recv()
                        value = value + recvs[half, way, s - 1].astype(F32)
                    sends[half, way, s] = value.astype(BF16)
                    copies[s].start()
                    pending.append(copies[s])

        def finish():
            total = block(7)
            for way, slots, copies in ways:
                copies[-1].wait_recv()
                total = total + recvs[half, way, len(slots) - 1].astype(F32)
            return total

        return step, finish

    dw_rings = [
        sum_ring(i, lambda slot, i=i: weight_block(slot, i), wsend, wrecv) for i in range(2)
    ]

    for copy in g_copies:
        copy.wait_recv()
    for r in range(4):
        block = gown[...] if r == 0 else gbuf[r]
        for h in range(2):
            gtall[:, r * 256 + h * 128 : r * 256 + h * 128 + 128] = block[
                h * 128 : h * 128 + 128, :
            ]
        stat = own_stat if r == 0 else gstatbuf[r]
        lanes = slice(r * 256, r * 256 + 256)
        frow[:, lanes] = jnp.exp2(mloc[:, lanes] - stat[0:1, :])
        drow[:, lanes] = stat[1:2, :]

    kv_sum_rings = [
        sum_ring(i, lambda slot, i=i: kvpart[i, slot * 128 : slot * 128 + 128, :], rsend, rrecv)
        for i in range(2)
    ]

    def backward(s):
        rows = slice(s * 256, s * 256 + 256)
        values = vrel[rows, :]
        for r in range(4):
            lanes = slice(r * 256, r * 256 + 256)
            grad_probs = nn(values, gtall[:, lanes])
            softmax = sp[rows, lanes] * frow[:, lanes]
            smp[:, lanes] = softmax.astype(BF16)
            dsb[rows, lanes] = (softmax * (grad_probs - drow[:, lanes])).astype(BF16)
        kvpart[0, rows, :] = nn(dsb[rows, :], qall[...]) * SCALE
        kvpart[1, rows, :] = nt(smp[...], gtall[...])

    backward(0)
    kv_sum_rings[0][0](0)
    backward(1)
    kv_sum_rings[1][0](0)
    for copy in (at_copies[1], at_copies[3], at_far[0], at_far[1]):
        copy.wait_recv()
    dwp[...] = nt(at[...], dot2[...])
    for step, _ in dw_rings:
        step(0)
    backward(2)
    backward(3)
    for s in range(1, 4):
        for step, _ in kv_sum_rings + dw_rings:
            step(s)

    dq_sem = sems.take(4)
    dq_copies = []
    for r in (1, 2, 3, 0):
        lanes = slice(r * 256, r * 256 + 256)
        part = nn(kt[...], dsb[:, lanes]) * SCALE
        if r == 0:
            dqown[...] = part
        else:
            k = 4 - r
            dqsend[r] = part.astype(BF16)
            dq_copies.append(
                sems.copy(dqsend.at[r], dqbuf.at[k], dq_sem + k, dq_sem + k, *group_peer(k))
            )
            dq_copies[-1].start()
    pending += dq_copies

    for i, (_, finish) in enumerate(kv_sum_rings):
        kvfin_send[i] = finish().T.astype(BF16)
    fin_send = sems.take(4)
    fin_recv = sems.take(4)
    source = lax.rem(yhi - key_quarter + 4, 4)
    fin_copies = []
    for k in range(4):
        column = lax.rem(m + k, 4)
        fin_copies.append(
            sems.copy(
                kvfin_send.at[:, pl.ds(pl.multiple_of(column * 32, 32), 32), :],
                kvfin.at[source],
                fin_send + k,
                fin_recv + source,
                g * 4 + column,
                key_quarter * 8 + z,
            )
        )
    for k in range(1, 4):
        fin_copies[k].start()
        pending.append(fin_copies[k])

    @pl.when(key_quarter != yhi)
    def _():
        fin_copies[0].start()

    @pl.when(key_quarter == yhi)
    def _():
        kvfin[0] = kvfin_send[:, pl.ds(pl.multiple_of(m * 32, 32), 32), :]

    for i, (_, finish) in enumerate(dw_rings):
        total = finish().astype(BF16)
        for y in range(2):
            dwsend[2 * i + y] = total[y * 80 : y * 80 + 80, :]
    dwf_sem = sems.take(4)
    dwf_copies = []
    for k in range(1, 4):
        dwf_copies.append(
            sems.copy(
                dwsend.at[lax.rem(yhi + k, 4)], dwfin.at[yhi], dwf_sem + k, dwf_sem + k, *y_peer(k)
            )
        )
        dwf_copies[-1].start()
    pending += dwf_copies
    dwfin[yhi] = dwsend[yhi]

    for copy in dq_copies:
        copy.wait_recv()
    query_grad = dqown[...]
    for k in range(1, 4):
        query_grad = query_grad + dqbuf[k].astype(F32)
    query_rows = jnp.concatenate([query_grad[:, :128], query_grad[:, 128:]], axis=0)
    dq_ref[...] = query_rows.T.astype(BF16)

    def fin_wait(s):
        sems.copy(
            kvfin_send.at[:, pl.ds(0, 32), :],
            kvfin.at[s],
            fin_send,
            fin_recv + s,
            *y_peer(1),
        ).wait_recv()

    for s in range(1, 4):
        fin_wait(s)

    @pl.when(key_quarter != yhi)
    def _():
        fin_wait(0)

    for i, out in ((0, dk_ref), (1, dv_ref)):
        total = kvfin[0, i].astype(F32)
        for s in range(1, 4):
            total = total + kvfin[s, i].astype(F32)
        out[...] = total.astype(BF16)

    for copy in dwf_copies:
        copy.wait_recv()
    columns = []
    blocks = [dwfin[q].astype(F32) for q in range(4)]
    for half in range(2):
        for pair in range(2):
            a, c = (
                [
                    blocks[2 * half + i][(pair * 5 + t) * 8 : (pair * 5 + t) * 8 + 8, :]
                    for t in range(5)
                ]
                for i in range(2)
            )
            columns += [
                a[0],
                a[1],
                join(a[2], turn(c[0])),
                join(turn(c[0]), turn(c[1])),
                join(turn(c[1]), turn(c[2])),
                join(turn(a[2]), turn(a[3])),
                join(turn(a[3]), turn(a[4])),
                join(turn(a[4]), c[2]),
                c[3],
                c[4],
            ]
    dw_ref[...] = jnp.concatenate(columns, axis=1).astype(BF16)

    for copy in pending:
        copy.wait_send()

    @pl.when(key_quarter == yhi)
    def _():
        for copy in kv_hop_copies:
            copy.wait_send()

    @pl.when(quarter != yhi)
    def _():
        turn_copy.wait_send()

    @pl.when(key_quarter != yhi)
    def _():
        fin_copies[0].wait_send()

    assert sems.used <= SEM_COUNT, sems.used


def deliver_kernel(*refs):
    count = len(refs) // 2
    for i in range(count):
        refs[count + i][...] = refs[i][...]


def deliver(results):
    vmem = pl.BlockSpec(memory_space=pltpu.VMEM)
    return pl.pallas_call(
        deliver_kernel,
        out_shape=[jax.ShapeDtypeStruct(r.shape, r.dtype) for r in results],
        in_specs=[vmem] * len(results),
        out_specs=[vmem] * len(results),
        compiler_params=pltpu.CompilerParams(vmem_limit_bytes=63 * 1024 * 1024),
    )(*results)


def per_device(block_order, query_states, key_states, value_states, out_weight, out_grad):
    v = pltpu.VMEM
    vmem = pl.BlockSpec(memory_space=pltpu.VMEM)
    scratch = [
        v((8, 5120), BF16),
        v((2, 128, 128), BF16),
        v((8, 2, 128, 128), BF16),
        v((4, 128, 256), BF16),
        v((1024, 128), BF16),
        v((1024, 128), BF16),
        v((1024, 128), BF16),
        v((128, 1024), BF16),
        v((128, 1024), BF16),
        v((4, 80, 128), BF16),
        v((8, 4, 80, 128), BF16),
        v((256, 1280), F32),
        v((320, 128), BF16),
        v((1280, 512), BF16),
        v((1024, 1024), F32),
        v((8, 1024), F32),
        v((1024, 1024), BF16),
        v((1024, 1024), BF16),
        v((1, 1024), F32),
        v((4, 128, 256), BF16),
        v((4, 128, 256), BF16),
        v((4, 8, 256), F32),
        v((4, 8, 256), F32),
        v((256, 512), BF16),
        v((256, 512), F32),
        v((4, 256, 128), BF16),
        v((4, 256, 128), BF16),
        v((256, 128), BF16),
        v((4, 256, 128), BF16),
        v((8, 256), F32),
        v((4, 8, 256), F32),
        v((128, 1024), BF16),
        v((1, 1024), F32),
        v((1, 1024), F32),
        v((256, 1024), BF16),
        v((2, 1024, 128), F32),
        v((2, 2, 4, 128, 128), BF16),
        v((2, 2, 4, 128, 128), BF16),
        v((2, 128, 128), BF16),
        v((4, 2, 32, 128), BF16),
        v((4, 128, 256), BF16),
        v((4, 128, 256), BF16),
        v((128, 256), F32),
        v((256, 1280), F32),
        v((2, 2, 4, 160, 128), BF16),
        v((2, 2, 4, 160, 128), BF16),
        v((4, 80, 128), BF16),
        v((4, 80, 128), BF16),
        pltpu.SemaphoreType.DMA((SEM_COUNT,)),
        pltpu.SemaphoreType.DMA((SEM_COUNT,)),
        pltpu.SemaphoreType.DMA((5,)),
    ]
    results = pl.pallas_call(
        kernel,
        out_shape=(
            jax.ShapeDtypeStruct((128, 256), BF16),
            jax.ShapeDtypeStruct((128, 256), BF16),
            jax.ShapeDtypeStruct((32, 128), BF16),
            jax.ShapeDtypeStruct((32, 128), BF16),
            jax.ShapeDtypeStruct((8, 5120), BF16),
        ),
        in_specs=[pl.BlockSpec(memory_space=pltpu.SMEM)] + [pl.BlockSpec(memory_space=pltpu.HBM)] * 5,
        out_specs=[vmem] * 5,
        scratch_shapes=scratch,
        compiler_params=pltpu.CompilerParams(
            collective_id=0, has_side_effects=True, vmem_limit_bytes=63 * 1024 * 1024
        ),
        cost_estimate=pl.CostEstimate(
            flops=2_500_000_000, bytes_accessed=1_000_000, transcendentals=1_100_000
        ),
    )(block_order, query_states, key_states, value_states, out_weight, out_grad.T)
    results = deliver(results)
    return results[0], results[1], results[2].T, results[3].T, results[4]


def solution(mesh):
    in_specs = (
        P(),
        P("ctx", "node"),
        P("ctx", None),
        P("ctx", None),
        P(("node", "ctx"), None),
        P("ctx", "node"),
    )
    out_specs = (
        P("ctx", "node"),
        P("ctx", "node"),
        P("ctx", "node"),
        P("ctx", "node"),
        P(("node", "ctx"), None),
    )
    return jax.shard_map(
        per_device, mesh=mesh, in_specs=in_specs, out_specs=out_specs, check_vma=False
    )
```
